128 devices in a mesh: expert: 16 (over z, x), helper: 8 (over y, core).
Axes of the slice: x: 4, y: 4, z: 4, core: 2. Of those that a mesh axis runs over, the one named last changes fastest.
Arguments:
- tokens: bfloat16 [8192, 4096], P(('expert', 'helper')), may hold values from -6 to 6
- expert_ids: int32 [8192, 8], P(('expert', 'helper')), may hold values from 0 to 127, all different within a row; in each aligned block of 64 rows (0 to 63, 64 to 127, ...) at most 5 rows name the same one
- gate_weights: float32 [8192, 8], P(('expert', 'helper')), may hold values from 0.05 to 1
- w_gate_up: bfloat16 [128, 4096, 2048], P(('expert', 'helper')), may hold values from -0.09375 to 0.09375
- gu_scales: float32 [128, 32, 16], P(('expert', 'helper')), may hold values from 0.5 to 2
- w_down: bfloat16 [128, 1024, 4096], P(('expert', 'helper')), may hold values from -0.1875 to 0.1875
- down_scales: float32 [128, 8, 32], P(('expert', 'helper')), may hold values from 0.5 to 2
Outputs:
- moe_out: bfloat16 [8192, 4096], P(('expert', 'helper'))
The draws below stay inside these ranges and needn't reach their ends.
Inputs may be any that keep to these rules, and one draw needn't show every extreme that they name: `expert_ids`: each row names 8 different experts; among the 64 rows of one device no expert is named by more than 5 rows, and in every draw some expert is named by exactly 5 rows of some device.
All inputs are finite; a program needn't handle non-finite values.
Results may differ from the reference program's by a relative error of at most 0.0076.
Values may be sent and summed in bfloat16 or wider, within the bound.
No kernel may reach another device: no remote copies, remote signals or barrier semaphores. Data moves between devices by JAX's collectives and lax.ppermute only.
A program may use at most 192 MiB of HBM per device.

```python
import math
import jax
import jax.numpy as jnp
import numpy as np
from jax import lax

D = 4096
FF = 1024
TOP = 8
QBLK = 128
TOK_DEV = 64
EXPERTS = 128
TOKENS = 8192
MOST = 5


def shard_levels(stream_key, dims, split, low, high):
    gain = 1.0
    for dim, parts in split:
        heights = jax.random.uniform(jax.random.fold_in(jax.random.fold_in(stream_key, 6), dim), (parts,), jnp.float32, low / len(split), high / len(split))
        gain = gain * jnp.repeat(jnp.exp(heights), dims[dim] // parts).reshape((-1,) + (1,) * (len(dims) - 1 - dim))
    return gain


def shared_out(key, own, number, rows, amount, top, reach, lean):
    sequence = jax.random.permutation(key, amount)
    crowded, common = shares(amount, rows * top, reach, lean, True), shares(amount, rows * top, reach, lean, False)
    places = jnp.arange(amount)

    def named(lengths, rotation):
        used = int((lengths > 0).sum())
        fixed = max(1, used // 4)
        passed = fixed + (places - fixed + rotation * (used - fixed)) % max(1, amount - fixed)
        return jnp.zeros((amount,), jnp.int32).at[sequence[jnp.where(places < fixed, places, passed)]].set(jnp.asarray(lengths, jnp.int32))

    lengths = jnp.where(number % 4 == 0, named(crowded, number // 4), named(common, number - number // 4 - 1))
    mixed = jax.random.permutation(jax.random.fold_in(own, 3), amount)
    donor, sink = mixed[0:amount // 2 * 2:2], mixed[1:amount // 2 * 2:2]
    room = jnp.minimum(lengths[donor] - 1, reach - lengths[sink]) // 2
    room = jnp.where((donor == sequence[0]) | (sink == sequence[0]) | (lengths[sink] == 0), 0, jnp.maximum(room, 0))
    passed = jax.random.randint(jax.random.fold_in(own, 4), (amount // 2,), 0, 1 << 20) % (room + 1)
    lengths = lengths.at[donor].add(-passed).at[sink].add(passed)
    members = jnp.searchsorted(jnp.cumsum(lengths), jnp.arange(rows * top), side="right").astype(jnp.int32)
    grid = members.reshape(top, rows).T
    grid = grid[jax.random.permutation(jax.random.fold_in(own, 1), rows)]
    rotation = jax.random.randint(jax.random.fold_in(own, 2), (rows, 1), 0, top)
    return jnp.take_along_axis(grid, (jnp.arange(top)[None, :] + rotation) % top, axis=1)


def shares(number_of, total, most, skew, full):
    portions = [(1 << 20) // math.isqrt(rank ** skew) + 1 for rank in range(1, number_of + 1)]
    largest = most if full else min(most, max(-(-total // number_of), total * portions[0] // sum(portions)))
    least = 1 if total - largest >= number_of - 1 else 0
    counts, surplus = [largest] + [least] * (number_of - 1), total - largest - least * (number_of - 1)
    while surplus > 0:
        movable = [i for i in range(1, number_of) if counts[i] < largest] or [i for i in range(1, number_of) if counts[i] < most]
        whole, remaining = sum([portions[i] for i in movable]), surplus
        for i in movable:
            extra = min(most - counts[i], max(1, remaining * portions[i] // whole), surplus)
            counts[i] = counts[i] + extra
            surplus = surplus - extra
    return np.array(counts)


def bell_draw(rng, shape, width, most, cuts=(), kind=jnp.bfloat16):
    array = width * jax.random.normal(rng, shape, jnp.float32)
    if cuts:
        array = array * shard_levels(rng, shape, cuts, -0.22, 0.18)
    return jnp.clip(array, -most, most).astype(kind)


def setup_inputs(seed: int = 0) -> dict:
    arg_keys = jax.random.split(jax.random.key(seed), 8)
    tokens = bell_draw(arg_keys[0], (TOKENS, D), 1.0, 6.0, ((0, 128),))
    expert_ids_keys = jax.random.split(jax.random.fold_in(arg_keys[1], 1), TOKENS // TOK_DEV)
    expert_ids_turns = jax.random.permutation(jax.random.fold_in(arg_keys[1], 3), TOKENS // TOK_DEV)
    expert_ids = jax.vmap(lambda own, number: shared_out(jax.random.fold_in(arg_keys[1], 2), own, number, TOK_DEV, EXPERTS, TOP, MOST, 2))(expert_ids_keys, expert_ids_turns).reshape((TOKENS, TOP))
    gate_weights = jnp.clip(jnp.exp(math.log(1.0) - 2.9957323 * jax.random.uniform(arg_keys[2], (TOKENS, TOP), jnp.float32) ** shard_levels(arg_keys[2], (TOKENS, TOP), ((0, 128),), -0.2, 0.2)), 0.05, 1.0)
    w_gate_up = bell_draw(arg_keys[3], (EXPERTS, D, 2 * FF), D ** -0.5, 0.09375, ((0, 128),))
    gu_scales = jnp.clip(jnp.exp(math.log(2.0) - 1.3862944 * jax.random.uniform(arg_keys[4], (EXPERTS, D // QBLK, 2 * FF // QBLK), jnp.float32) ** shard_levels(arg_keys[4], (EXPERTS, D // QBLK, 2 * FF // QBLK), ((0, 128),), -0.2, 0.2)), 0.5, 2.0)
    w_down = bell_draw(arg_keys[5], (EXPERTS, FF, D), FF ** -0.5, 0.1875, ((0, 128),))
    down_scales = jnp.clip(jnp.exp(math.log(2.0) - 1.3862944 * jax.random.uniform(arg_keys[6], (EXPERTS, FF // QBLK, D // QBLK), jnp.float32) ** shard_levels(arg_keys[6], (EXPERTS, FF // QBLK, D // QBLK), ((0, 128),), -0.2, 0.2)), 0.5, 2.0)
    return {"tokens": tokens, "expert_ids": expert_ids, "gate_weights": gate_weights, "w_gate_up": w_gate_up, "gu_scales": gu_scales, "w_down": w_down, "down_scales": down_scales}


def dequant(weight, scales):
    row_count, col_count = weight.shape
    blocked = weight.astype(jnp.float32).reshape(row_count // QBLK, QBLK, col_count // QBLK, QBLK)
    return (blocked * scales[:, None, :, None]).reshape(row_count, col_count).astype(jnp.bfloat16)


def expert_rows(inputs, gate_up_deq, down_deq):
    pre_act = jnp.dot(inputs, gate_up_deq, preferred_element_type=jnp.float32)
    hidden_units = down_deq.shape[0]
    hidden = (jax.nn.silu(pre_act[:, :hidden_units]) * pre_act[:, hidden_units:]).astype(jnp.bfloat16)
    return jnp.dot(hidden, down_deq, preferred_element_type=jnp.float32).astype(jnp.bfloat16)


def reference(tokens, expert_ids, gate_weights, w_gate_up, gu_scales, w_down, down_scales):
    sources = TOKENS // TOK_DEV
    src_assign = TOK_DEV * TOP
    mix_weights = gate_weights / jnp.sum(gate_weights, axis=1, keepdims=True)
    flat_ids = expert_ids.reshape(sources, src_assign).astype(jnp.int32)
    onehot = (flat_ids[:, :, None] == jnp.arange(EXPERTS, dtype=jnp.int32)[None, None, :]).astype(jnp.int32)
    rank_in = jnp.sum((jnp.cumsum(onehot, axis=1) - 1) * onehot, axis=2).astype(jnp.int32)
    src_index = jnp.arange(sources, dtype=jnp.int32)[:, None]
    column = (src_index * MOST + rank_in).astype(jnp.int32)
    tok_index = (src_index * TOK_DEV + jnp.arange(src_assign, dtype=jnp.int32)[None, :] // TOP).astype(jnp.int32)
    capacity = sources * MOST
    tok_table = jnp.full((EXPERTS, capacity), TOKENS, jnp.int32).at[flat_ids, column].set(tok_index)
    wgt_table = jnp.zeros((EXPERTS, capacity), jnp.float32).at[flat_ids, column].set(mix_weights.reshape(sources, src_assign))
    padded = jnp.concatenate([tokens, jnp.zeros((1, D), tokens.dtype)], axis=0)

    def one_expert(running, inputs):
        token_index, weight_col, wgu, sgu, wdn, sdn = inputs
        outputs = expert_rows(padded[token_index], dequant(wgu, sgu), dequant(wdn, sdn))
        running = running.at[token_index].add(weight_col[:, None] * outputs.astype(jnp.float32))
        return running, None

    start_sum = jnp.zeros((TOKENS + 1, D), jnp.float32)
    running, _ = lax.scan(one_expert, start_sum, (tok_table, wgt_table, w_gate_up, gu_scales, w_down, down_scales))
    return running[:TOKENS].astype(jnp.bfloat16)
```

```python
import functools

import jax
import jax.numpy as jnp
from jax import lax
from jax.experimental import pallas as pl
from jax.experimental.pallas import tpu as pltpu
from jax.sharding import PartitionSpec as P

QBLK = 128
SLOTS = 5
ROWS = 8
EXTRA = ROWS - SLOTS
MIB = 1 << 20


def iota(shape, dim):
    return lax.broadcasted_iota(jnp.int32, shape, dim)


def slots_of(ids, experts):
    tok_rows, route_count = ids.shape
    expert_of = iota((tok_rows, experts), 1)
    hit = jnp.zeros((tok_rows, experts), jnp.float32)
    for k in range(route_count):
        hit = hit + jnp.where(ids[:, k : k + 1] == expert_of, 1.0, 0.0)
    earlier = jnp.where(iota((tok_rows, tok_rows), 0) > iota((tok_rows, tok_rows), 1), 1.0, 0.0)
    rank = jnp.dot(
        earlier.astype(jnp.bfloat16), hit.astype(jnp.bfloat16), preferred_element_type=jnp.float32
    )
    return jnp.where(hit > 0.5, rank, -1.0)


def pack_kernel(ids_ref, tok_ref, out_ref, slot_ref):
    step = pl.program_id(0)
    tok_rows, feat_width = tok_ref.shape
    block_rows, group_width = out_ref.shape
    experts = block_rows // ROWS
    parts = 1 + EXTRA
    shape = (block_rows, parts * tok_rows)
    row = iota(shape, 0) % ROWS

    @pl.when(step == 0)
    def _():
        slot = slots_of(ids_ref[...], experts).astype(jnp.bfloat16)
        repeat = jnp.where(
            iota((block_rows, experts), 0) // ROWS == iota((block_rows, experts), 1), 1.0, 0.0
        ).astype(jnp.bfloat16)
        spread = lax.dot_general(
            repeat,
            jnp.concatenate([slot] * parts, axis=0),
            (((1,), (1,)), ((), ())),
            preferred_element_type=jnp.float32,
        )
        part = iota(shape, 1) // tok_rows
        slot_ref[...] = jnp.where(jnp.maximum(row - (SLOTS - 1), 0) == part, spread, -1.0)

    want = jnp.where(row < SLOTS, row, step).astype(jnp.float32)
    chosen = jnp.where(slot_ref[...] == want, 1.0, 0.0).astype(jnp.bfloat16)
    start = pl.multiple_of(step * group_width, group_width)
    source = jnp.concatenate(
        [tok_ref[:, pl.ds(start, group_width)]]
        + [tok_ref[:, f * group_width : (f + 1) * group_width] for f in range(SLOTS, ROWS)],
        axis=0,
    )
    out_ref[...] = jnp.dot(chosen, source, preferred_element_type=jnp.float32).astype(out_ref.dtype)


def pack(tokens, expert_ids, experts):
    tok_rows, feat_width = tokens.shape
    group_width = feat_width // ROWS
    block_rows = experts * ROWS
    return pl.pallas_call(
        pack_kernel,
        grid=(SLOTS,),
        out_shape=jax.ShapeDtypeStruct((block_rows, SLOTS * group_width), tokens.dtype),
        in_specs=[
            pl.BlockSpec(expert_ids.shape, lambda i: (0, 0)),
            pl.BlockSpec(tokens.shape, lambda i: (0, 0)),
        ],
        out_specs=pl.BlockSpec((block_rows, group_width), lambda i: (0, i)),
        scratch_shapes=[pltpu.VMEM((block_rows, (1 + EXTRA) * tok_rows), jnp.float32)],
        compiler_params=pltpu.CompilerParams(vmem_limit_bytes=32 * MIB),
        name="pack",
    )(expert_ids, tokens)


def plan_kernel(ids_ref, gate_ref, out_ref):
    step = pl.program_id(0)
    tok_rows, route_count = ids_ref.shape
    block_rows = out_ref.shape[-1]
    experts = block_rows // ROWS
    gates = gate_ref[...]
    mix = gates / jnp.sum(gates, axis=1, keepdims=True)
    slot = slots_of(ids_ref[...], experts)
    expert_of = iota((tok_rows, experts), 1)
    mix_of = jnp.zeros((tok_rows, experts), jnp.float32)
    for k in range(route_count):
        mix_of = mix_of + jnp.where(ids_ref[:, k : k + 1] == expert_of, mix[:, k : k + 1], 0.0)
    high = mix_of.astype(jnp.bfloat16)
    low = (mix_of - high.astype(jnp.float32)).astype(jnp.bfloat16)
    repeat = jnp.where(
        iota((experts, block_rows), 1) // ROWS == iota((experts, block_rows), 0), 1.0, 0.0
    ).astype(jnp.bfloat16)
    spread = jnp.dot(slot.astype(jnp.bfloat16), repeat, preferred_element_type=jnp.float32)
    row = iota((tok_rows, block_rows), 1) % ROWS
    for half, piece in enumerate((high, low)):
        weight = jnp.dot(piece, repeat, preferred_element_type=jnp.float32)
        for part in range(1 + EXTRA):
            if part == 0:
                keep = (row < SLOTS) & (spread == row.astype(jnp.float32))
            else:
                keep = (row == SLOTS - 1 + part) & (spread == step.astype(jnp.float32))
            first = (half * (1 + EXTRA) + part) * tok_rows
            out_ref[0, first : first + tok_rows, :] = jnp.where(keep, weight, 0.0).astype(jnp.bfloat16)


def plan(expert_ids, gate_weights, experts):
    tok_rows = expert_ids.shape[0]
    shape = (2 * (1 + EXTRA) * tok_rows, experts * ROWS)
    return pl.pallas_call(
        plan_kernel,
        grid=(SLOTS,),
        out_shape=jax.ShapeDtypeStruct((SLOTS,) + shape, jnp.bfloat16),
        in_specs=[
            pl.BlockSpec(expert_ids.shape, lambda i: (0, 0)),
            pl.BlockSpec(gate_weights.shape, lambda i: (0, 0)),
        ],
        out_specs=pl.BlockSpec((1,) + shape, lambda i: (i, 0, 0)),
        compiler_params=pltpu.CompilerParams(vmem_limit_bytes=32 * MIB),
        cost_estimate=pl.CostEstimate(flops=10**9, bytes_accessed=6 * 10**6, transcendentals=0),
        name="plan",
    )(expert_ids, gate_weights)


def dequant_kernel(scale_ref, weight_ref, out_ref):
    row_blocks, col_blocks = (n // QBLK for n in weight_ref.shape)
    first_row = pl.program_id(0) * row_blocks
    first_col = pl.program_id(1) * col_blocks
    for i in range(row_blocks):
        for j in range(col_blocks):
            here = (slice(i * QBLK, (i + 1) * QBLK), slice(j * QBLK, (j + 1) * QBLK))
            scale = scale_ref[first_row + i, first_col + j]
            out_ref[here] = (weight_ref[here].astype(jnp.float32) * scale).astype(out_ref.dtype)


def dequant(weight, scales, block, place):
    row_count, col_count = weight.shape
    return pl.pallas_call(
        dequant_kernel,
        grid=(row_count // block[0], col_count // block[1]),
        out_shape=jax.ShapeDtypeStruct(weight.shape, weight.dtype),
        in_specs=[
            pl.BlockSpec(memory_space=pltpu.SMEM),
            pl.BlockSpec(block, lambda i, j: (i, j)),
        ],
        out_specs=pl.BlockSpec(block, lambda i, j: (i, place(j))),
        compiler_params=pltpu.CompilerParams(vmem_limit_bytes=32 * MIB),
        cost_estimate=pl.CostEstimate(
            flops=row_count * col_count, bytes_accessed=4 * row_count * col_count, transcendentals=0
        ),
        name="dequant",
    )(scales, weight)


def expert_kernel(
    steps_up, sources, in_ref, gu_ref, down_ref, out_ref, x_ref, hidden_ref, extra_ref
):
    step = pl.program_id(0)
    group_width = out_ref.shape[1]
    hidden_tile = gu_ref.shape[1] // 2
    span = sources * ROWS
    kept = sources * SLOTS
    runs = in_ref.shape[0] // span

    def turned(back):
        to, come = iota((span, span), 1 if back else 0), iota((span, span), 0 if back else 1)
        same = (to // sources == come % ROWS) & (to % sources == come // ROWS)
        return jnp.where(same, 1.0, 0.0).astype(jnp.bfloat16)

    @pl.when(step == 0)
    def _():
        order = turned(False)
        for run in range(runs):
            for group in range(SLOTS):
                cols = slice(group * group_width, (group + 1) * group_width)
                moved = jnp.dot(
                    order,
                    in_ref[run * span : (run + 1) * span, cols],
                    preferred_element_type=jnp.float32,
                ).astype(x_ref.dtype)
                for row in range(ROWS):
                    slot, feature = (row, group) if row < SLOTS else (group, row)
                    first = run * kept + slot * sources
                    x_ref[
                        first : first + sources, feature * group_width : (feature + 1) * group_width
                    ] = moved[row * sources : (row + 1) * sources]

    @pl.when(step < steps_up)
    def _():
        pre = jnp.dot(x_ref[...], gu_ref[...], preferred_element_type=jnp.float32)
        gate, up = pre[:, :hidden_tile], pre[:, hidden_tile:]
        start = pl.multiple_of(step * hidden_tile, hidden_tile)
        hidden_ref[:, pl.ds(start, hidden_tile)] = (gate / (1.0 + jnp.exp(-gate)) * up).astype(
            hidden_ref.dtype
        )

    def product():
        return jnp.dot(
            hidden_ref[...], down_ref[...], preferred_element_type=jnp.float32
        ).astype(jnp.bfloat16)

    @pl.when((step >= steps_up) & (step < steps_up + EXTRA))
    def _():
        extra_ref[step - steps_up] = product()

    @pl.when(step >= steps_up + EXTRA)
    def _():
        result = product()
        group = step - (steps_up + EXTRA)
        order = turned(True)
        for run in range(runs):
            start = pl.multiple_of(run * kept + group * sources, sources)
            gathered = jnp.concatenate(
                [result[run * kept : (run + 1) * kept]]
                + [extra_ref[i, pl.ds(start, sources), :] for i in range(EXTRA)],
                axis=0,
            )
            out_ref[run * span : (run + 1) * span, :] = jnp.dot(
                order, gathered, preferred_element_type=jnp.float32
            ).astype(out_ref.dtype)


def expert(arrived, gate_up, down, hidden_tile):
    block_rows, packed_width = arrived.shape
    feat_width, hidden_width = gate_up.shape[0], down.shape[0]
    group_width = feat_width // ROWS
    live_rows = block_rows // ROWS * SLOTS
    steps_up = hidden_width // hidden_tile
    last_up = steps_up - 1

    def feature(i):
        return (jnp.maximum(i - steps_up, 0) + SLOTS) % ROWS

    return pl.pallas_call(
        functools.partial(expert_kernel, steps_up, 256 // ROWS),
        grid=(steps_up + ROWS,),
        out_shape=jax.ShapeDtypeStruct(arrived.shape, arrived.dtype),
        in_specs=[
            pl.BlockSpec(arrived.shape, lambda i: (0, 0)),
            pl.BlockSpec((feat_width, 2 * hidden_tile), lambda i: (0, jnp.minimum(i, last_up))),
            pl.BlockSpec((hidden_width, group_width), lambda i: (0, feature(i))),
        ],
        out_specs=pl.BlockSpec(
            (block_rows, group_width), lambda i: (0, jnp.maximum(i - steps_up - EXTRA, 0))
        ),
        scratch_shapes=[
            pltpu.VMEM((live_rows, feat_width), jnp.bfloat16),
            pltpu.VMEM((live_rows, hidden_width), jnp.bfloat16),
            pltpu.VMEM((EXTRA, live_rows, group_width), jnp.bfloat16),
        ],
        compiler_params=pltpu.CompilerParams(vmem_limit_bytes=56 * MIB),
        cost_estimate=pl.CostEstimate(
            flops=2 * live_rows * 3 * feat_width * hidden_width,
            bytes_accessed=6 * feat_width * hidden_width + 4 * block_rows * packed_width,
            transcendentals=live_rows * hidden_width,
        ),
        name="expert",
    )(arrived, gate_up, down)


def combine_kernel(weight_ref, in_ref, out_ref, total_ref):
    step = pl.program_id(0)
    tok_rows = out_ref.shape[0]
    group_width = in_ref.shape[1]
    half = weight_ref.shape[1] // 2
    both = jnp.dot(weight_ref[0], in_ref[...], preferred_element_type=jnp.float32)
    part = both[:half] + both[half:]
    start = pl.multiple_of(step * group_width, group_width)
    out_ref[:, pl.ds(start, group_width)] = part[:tok_rows].astype(out_ref.dtype)

    @pl.when(step == 0)
    def _():
        total_ref[...] = part[tok_rows:]

    @pl.when(step > 0)
    def _():
        total_ref[...] += part[tok_rows:]

    @pl.when(step == SLOTS - 1)
    def _():
        for i in range(EXTRA):
            cols = slice((SLOTS + i) * group_width, (SLOTS + i + 1) * group_width)
            out_ref[:, cols] = total_ref[i * tok_rows : (i + 1) * tok_rows].astype(out_ref.dtype)


def combine(weights, returned, out_shape):
    group_width = out_shape.shape[1] // ROWS
    return pl.pallas_call(
        combine_kernel,
        grid=(SLOTS,),
        out_shape=out_shape,
        in_specs=[
            pl.BlockSpec((1,) + weights.shape[1:], lambda i: (i, 0, 0)),
            pl.BlockSpec((returned.shape[0], group_width), lambda i: (0, i)),
        ],
        out_specs=pl.BlockSpec(out_shape.shape, lambda i: (0, 0)),
        scratch_shapes=[pltpu.VMEM((EXTRA * out_shape.shape[0], group_width), jnp.float32)],
        compiler_params=pltpu.CompilerParams(vmem_limit_bytes=32 * MIB),
        name="combine",
    )(weights, returned)


def exchange(blocks, experts):
    shape = blocks.shape
    moved = lax.all_to_all(
        blocks.reshape(experts, ROWS, shape[1]),
        ("expert", "helper"),
        split_axis=0,
        concat_axis=0,
        tiled=True,
    )
    return moved.reshape(shape)


def shards(tokens, expert_ids, gate_weights, w_gate_up, gu_scales, w_down, down_scales):
    experts = lax.axis_size("expert") * lax.axis_size("helper")
    hidden_width = w_down.shape[1]
    tile = 256
    tiles = hidden_width // tile
    arrived = exchange(pack(tokens, expert_ids, experts), experts)
    gate_up = dequant(
        w_gate_up[0], gu_scales[0], (1024, tile), lambda j: 2 * (j % tiles) + j // tiles
    )
    down = dequant(w_down[0], down_scales[0], (256, 1024), lambda j: j)
    weights = plan(expert_ids, gate_weights, experts)
    returned = exchange(expert(arrived, gate_up, down, tile), experts)
    return combine(weights, returned, jax.ShapeDtypeStruct(tokens.shape, tokens.dtype))


def solution(mesh):
    rows = ("expert", "helper")
    placed = (P(rows, None),) * 3 + (P(rows, None, None),) * 4
    return jax.shard_map(
        shards, mesh=mesh, in_specs=placed, out_specs=P(rows, None), check_vma=False
    )
```

```python
import functools

import jax
import jax.numpy as jnp
from jax import lax
from jax.experimental import pallas as pl
from jax.experimental.pallas import tpu as pltpu
from jax.sharding import PartitionSpec as P

QBLK = 128
SLOTS = 5
ROWS = 8
EXTRA = ROWS - SLOTS
MIB = 1 << 20


def iota(shape, dim):
    return lax.broadcasted_iota(jnp.int32, shape, dim)


def slots_of(ids, experts):
    tok_rows, route_count = ids.shape
    expert_of = iota((tok_rows, experts), 1)
    hit = jnp.zeros((tok_rows, experts), jnp.float32)
    for k in range(route_count):
        hit = hit + jnp.where(ids[:, k : k + 1] == expert_of, 1.0, 0.0)
    earlier = jnp.where(iota((tok_rows, tok_rows), 0) > iota((tok_rows, tok_rows), 1), 1.0, 0.0)
    rank = jnp.dot(
        earlier.astype(jnp.bfloat16), hit.astype(jnp.bfloat16), preferred_element_type=jnp.float32
    )
    return jnp.where(hit > 0.5, rank, -1.0)


def slots_for(ids, experts):
    route_count, tok_rows = ids.shape
    expert_of = iota((experts, tok_rows), 0)
    hit = jnp.zeros((experts, tok_rows), jnp.float32)
    for k in range(route_count):
        hit = hit + jnp.where(ids[k : k + 1, :] == expert_of, 1.0, 0.0)
    earlier = jnp.where(iota((tok_rows, tok_rows), 0) < iota((tok_rows, tok_rows), 1), 1.0, 0.0)
    rank = jnp.dot(
        hit.astype(jnp.bfloat16), earlier.astype(jnp.bfloat16), preferred_element_type=jnp.float32
    )
    return jnp.where(hit > 0.5, rank, -1.0)


ALWAYS = 99.0


def pack_kernel(ids_ref, given_ref, out_ref, tok_ref, block_ref, slot_ref, tok_sem, out_sem):
    tok_rows, feat_width = tok_ref.shape
    group_width = feat_width // ROWS
    block_rows = block_ref.shape[0]
    experts = block_rows // ROWS
    parts = 1 + EXTRA
    fetch = pltpu.make_async_copy(given_ref, tok_ref, tok_sem)
    fetch.start()

    slot = slots_for(ids_ref[...], experts).astype(jnp.bfloat16)
    repeat = jnp.where(
        iota((block_rows, experts), 0) // ROWS == iota((block_rows, experts), 1), 1.0, 0.0
    ).astype(jnp.bfloat16)
    spread = jnp.dot(
        repeat, jnp.concatenate([slot] * parts, axis=1), preferred_element_type=jnp.float32
    )
    shape = (block_rows, parts * tok_rows)
    row = iota(shape, 0) % ROWS
    part = iota(shape, 1) // tok_rows
    own = (part == 0) & (row.astype(jnp.float32) == spread) & (row < SLOTS)
    shared = (part > 0) & (row == SLOTS - 1 + part)
    slot_ref[...] = jnp.where(own, ALWAYS, jnp.where(shared, spread, -1.0))
    fetch.wait()

    def group(g):
        return slice(g * group_width, (g + 1) * group_width)

    writes = []
    for g in range(SLOTS):
        code = slot_ref[...]
        chosen = jnp.where((code == ALWAYS) | (code == float(g)), 1.0, 0.0).astype(jnp.bfloat16)
        source = jnp.concatenate(
            [tok_ref[:, group(f)] for f in (g, *range(SLOTS, ROWS))], axis=0
        )
        block_ref[:, group(g)] = jnp.dot(
            chosen, source, preferred_element_type=jnp.float32
        ).astype(block_ref.dtype)
        writes.append(
            pltpu.make_async_copy(block_ref.at[:, group(g)], out_ref.at[:, group(g)], out_sem.at[g])
        )
        writes[-1].start()
    for write in writes:
        write.wait()


def pack(tokens, expert_ids, experts):
    tok_rows, feat_width = tokens.shape
    shape = (experts * ROWS, feat_width // ROWS * SLOTS)
    return pl.pallas_call(
        pack_kernel,
        out_shape=pltpu.HBM(shape, tokens.dtype),
        in_specs=[pl.BlockSpec(memory_space=pltpu.VMEM), pl.BlockSpec(memory_space=pl.ANY)],
        out_specs=pl.BlockSpec(memory_space=pl.ANY),
        scratch_shapes=[
            pltpu.VMEM(tokens.shape, tokens.dtype),
            pltpu.VMEM(shape, tokens.dtype),
            pltpu.VMEM((shape[0], (1 + EXTRA) * tok_rows), jnp.float32),
            pltpu.SemaphoreType.DMA,
            pltpu.SemaphoreType.DMA((SLOTS,)),
        ],
        compiler_params=pltpu.CompilerParams(vmem_limit_bytes=32 * MIB),
        name="pack",
    )(expert_ids.T, pltpu.with_memory_space_constraint(tokens, pltpu.HBM))


def plan_kernel(ids_ref, gate_ref, slot_ref, mix_ref):
    tok_rows, route_count = ids_ref.shape
    block_rows = slot_ref.shape[1]
    experts = block_rows // ROWS
    gates = gate_ref[...]
    mix = gates / jnp.sum(gates, axis=1, keepdims=True)
    slot = slots_of(ids_ref[...], experts)
    expert_of = iota((tok_rows, experts), 1)
    mix_of = jnp.zeros((tok_rows, experts), jnp.float32)
    for k in range(route_count):
        mix_of = mix_of + jnp.where(ids_ref[:, k : k + 1] == expert_of, mix[:, k : k + 1], 0.0)
    repeat = jnp.where(
        iota((experts, block_rows), 1) // ROWS == iota((experts, block_rows), 0), 1.0, 0.0
    ).astype(jnp.bfloat16)
    slot_ref[...] = jnp.dot(slot.astype(jnp.bfloat16), repeat, preferred_element_type=jnp.float32)
    mix_ref[...] = jnp.dot(
        mix_of.astype(jnp.bfloat16), repeat, preferred_element_type=jnp.float32
    )


def plan(expert_ids, gate_weights, experts):
    shape = (expert_ids.shape[0], experts * ROWS)
    return pl.pallas_call(
        plan_kernel,
        out_shape=(pltpu.HBM(shape, jnp.float32), pltpu.HBM(shape, jnp.float32)),
        compiler_params=pltpu.CompilerParams(vmem_limit_bytes=16 * MIB),
        cost_estimate=pl.CostEstimate(flops=10**8, bytes_accessed=10**6, transcendentals=0),
        name="plan",
    )(expert_ids, gate_weights)


def dequant_kernel(place, scale_ref, weight_ref, out_ref):
    row_blocks, col_blocks = (n // QBLK for n in weight_ref.shape)
    step = pl.program_id(0)
    for i in range(row_blocks):
        rows = slice(i * QBLK, (i + 1) * QBLK)
        for j in range(col_blocks):
            scale = scale_ref[step * row_blocks + i, j]
            scaled = weight_ref[rows, j * QBLK : (j + 1) * QBLK].astype(jnp.float32) * scale
            out_ref[rows, place(j) * QBLK : (place(j) + 1) * QBLK] = scaled.astype(out_ref.dtype)


def dequant(weight, scales, rows, place):
    row_count, col_count = weight.shape
    block = pl.BlockSpec((rows, col_count), lambda i: (i, 0))
    return pl.pallas_call(
        functools.partial(dequant_kernel, place),
        grid=(row_count // rows,),
        out_shape=pltpu.HBM(weight.shape, weight.dtype),
        in_specs=[pl.BlockSpec(memory_space=pltpu.SMEM), block],
        out_specs=block,
        compiler_params=pltpu.CompilerParams(vmem_limit_bytes=16 * MIB),
        cost_estimate=pl.CostEstimate(
            flops=row_count * col_count, bytes_accessed=4 * row_count * col_count, transcendentals=0
        ),
        name="dequant",
    )(scales, pltpu.with_memory_space_constraint(weight, pltpu.HBM))


def expert_kernel(
    hidden_tile, given_ref, gu_given_ref, down_given_ref, out_ref,
    in_ref, gu_ref, down_ref, x_ref, hidden_ref, extra_ref, result_ref,
    in_sem, gu_sem, down_sem, out_sem,
):
    step = pl.program_id(0)
    group_width = result_ref.shape[2]
    runs, tiles = in_sem.shape[0], gu_sem.shape[0]
    span = in_ref.shape[0] // runs
    sources = span // ROWS
    kept = sources * SLOTS
    up_end = runs + tiles
    per_tile = ROWS // tiles

    def in_copy(run):
        rows = pl.ds(pl.multiple_of(run * span, span), span)
        return pltpu.make_async_copy(given_ref.at[rows], in_ref.at[rows], in_sem.at[run])

    def gu_copy(tile):
        cols = pl.ds(pl.multiple_of(tile * 2 * hidden_tile, 2 * hidden_tile), 2 * hidden_tile)
        return pltpu.make_async_copy(gu_given_ref.at[:, cols], gu_ref.at[:, cols], gu_sem.at[tile])

    def down_copy(turn):
        cols = pl.ds(pl.multiple_of((turn + SLOTS) % ROWS * group_width, group_width), group_width)
        return pltpu.make_async_copy(
            down_given_ref.at[:, cols], down_ref.at[:, cols], down_sem.at[turn]
        )

    def out_copy(group):
        cols = pl.ds(pl.multiple_of(group * group_width, group_width), group_width)
        return pltpu.make_async_copy(result_ref.at[group], out_ref.at[:, cols], out_sem.at[group])

    @pl.when(step == 0)
    def _():
        for run in range(runs):
            in_copy(run).start()
        gu_copy(0).start()

    @pl.when((step >= runs) & (step < up_end))
    def _():
        tile = step - runs
        gu_copy(tile).wait()

        @pl.when(tile + 1 < tiles)
        def _():
            gu_copy(tile + 1).start()

        for i in range(per_tile):
            down_copy(tile * per_tile + i).start()

    @pl.when(step < runs)
    def _():
        in_copy(step).wait()

    @pl.when(step >= up_end)
    def _():
        down_copy(step - up_end).wait()

    def turned(back):
        to, come = iota((span, span), 1 if back else 0), iota((span, span), 0 if back else 1)
        same = (to // sources == come % ROWS) & (to % sources == come // ROWS)
        return jnp.where(same, 1.0, 0.0).astype(jnp.bfloat16)

    @pl.when(step < runs)
    def _():
        order = turned(False)
        base = pl.multiple_of(step * kept, kept)
        rows = pl.ds(pl.multiple_of(step * span, span), span)
        for group in range(SLOTS):
            moved = jnp.dot(
                order,
                in_ref[rows, group * group_width : (group + 1) * group_width],
                preferred_element_type=jnp.float32,
            ).astype(x_ref.dtype)
            for row in range(ROWS):
                slot, feature = (row, group) if row < SLOTS else (group, row)
                x_ref[
                    pl.ds(base + slot * sources, sources),
                    feature * group_width : (feature + 1) * group_width,
                ] = moved[row * sources : (row + 1) * sources]

    @pl.when((step >= runs) & (step < up_end))
    def _():
        tile = step - runs
        both = pl.ds(pl.multiple_of(tile * 2 * hidden_tile, 2 * hidden_tile), 2 * hidden_tile)
        pre = jnp.dot(x_ref[...], gu_ref[:, both], preferred_element_type=jnp.float32)
        gate, up = pre[:, :hidden_tile], pre[:, hidden_tile:]
        start = pl.multiple_of(tile * hidden_tile, hidden_tile)
        hidden_ref[:, pl.ds(start, hidden_tile)] = (gate / (1.0 + jnp.exp(-gate)) * up).astype(
            hidden_ref.dtype
        )

    def product(feature):
        cols = pl.ds(pl.multiple_of(feature * group_width, group_width), group_width)
        return jnp.dot(
            hidden_ref[...], down_ref[:, cols], preferred_element_type=jnp.float32
        ).astype(jnp.bfloat16)

    @pl.when((step >= up_end) & (step < up_end + EXTRA))
    def _():
        extra_ref[step - up_end] = product(step - up_end + SLOTS)

    @pl.when(step >= up_end + EXTRA)
    def _():
        group = step - (up_end + EXTRA)
        result = product(group)
        order = turned(True)
        for run in range(runs):
            start = pl.multiple_of(run * kept + group * sources, sources)
            gathered = jnp.concatenate(
                [result[run * kept : (run + 1) * kept]]
                + [extra_ref[i, pl.ds(start, sources), :] for i in range(EXTRA)],
                axis=0,
            )
            result_ref[group, run * span : (run + 1) * span, :] = jnp.dot(
                order, gathered, preferred_element_type=jnp.float32
            ).astype(result_ref.dtype)
        out_copy(group).start()

    @pl.when(step == up_end + ROWS - 1)
    def _():
        for group in range(SLOTS):
            out_copy(group).wait()


def expert(arrived, gate_up, down, hidden_tile):
    block_rows, packed_width = arrived.shape
    feat_width, hidden_width = gate_up.shape[0], down.shape[0]
    group_width = feat_width // ROWS
    live_rows = block_rows // ROWS * SLOTS
    runs = block_rows // 256
    tiles = hidden_width // hidden_tile
    given = pl.BlockSpec(memory_space=pl.ANY)

    return pl.pallas_call(
        functools.partial(expert_kernel, hidden_tile),
        grid=(runs + tiles + ROWS,),
        out_shape=pltpu.HBM(arrived.shape, arrived.dtype),
        in_specs=[given, given, given],
        out_specs=given,
        scratch_shapes=[
            pltpu.VMEM(arrived.shape, jnp.bfloat16),
            pltpu.VMEM(gate_up.shape, jnp.bfloat16),
            pltpu.VMEM(down.shape, jnp.bfloat16),
            pltpu.VMEM((live_rows, feat_width), jnp.bfloat16),
            pltpu.VMEM((live_rows, hidden_width), jnp.bfloat16),
            pltpu.VMEM((EXTRA, live_rows, group_width), jnp.bfloat16),
            pltpu.VMEM((SLOTS, block_rows, group_width), jnp.bfloat16),
            pltpu.SemaphoreType.DMA((runs,)),
            pltpu.SemaphoreType.DMA((tiles,)),
            pltpu.SemaphoreType.DMA((ROWS,)),
            pltpu.SemaphoreType.DMA((SLOTS,)),
        ],
        compiler_params=pltpu.CompilerParams(vmem_limit_bytes=56 * MIB),
        cost_estimate=pl.CostEstimate(
            flops=2 * live_rows * 3 * feat_width * hidden_width,
            bytes_accessed=6 * feat_width * hidden_width + 4 * block_rows * packed_width,
            transcendentals=live_rows * hidden_width,
        ),
        name="expert",
    )(*(pltpu.with_memory_space_constraint(a, pltpu.HBM) for a in (arrived, gate_up, down)))


def combine_kernel(
    slot_given_ref, mix_given_ref, given_ref, out_ref,
    slot_ref, mix_ref, in_ref, weight_ref, slot_sem, mix_sem, in_sem,
):
    tok_rows, feat_width = out_ref.shape
    group_width = feat_width // ROWS

    def group(g):
        return slice(g * group_width, (g + 1) * group_width)

    plans = [
        pltpu.make_async_copy(slot_given_ref, slot_ref, slot_sem),
        pltpu.make_async_copy(mix_given_ref, mix_ref, mix_sem),
    ]
    reads = [
        pltpu.make_async_copy(given_ref.at[:, group(g)], in_ref.at[:, group(g)], in_sem.at[g])
        for g in range(SLOTS)
    ]
    for copy in plans + reads:
        copy.start()
    for copy in plans:
        copy.wait()
    slot, mix = slot_ref[...], mix_ref[...]
    row = iota(slot.shape, 1) % ROWS
    own = jnp.where((row < SLOTS) & (slot == row.astype(jnp.float32)), mix, 0.0)
    own = own.astype(weight_ref.dtype)
    for g in range(SLOTS):
        weight_ref[g, :tok_rows] = own
        here = jnp.where(slot == float(g), mix, 0.0)
        for i in range(EXTRA):
            weight_ref[g, (1 + i) * tok_rows : (2 + i) * tok_rows] = jnp.where(
                row == SLOTS + i, here, 0.0
            ).astype(weight_ref.dtype)
    total = jnp.zeros((EXTRA * tok_rows, group_width), jnp.float32)
    for g in range(SLOTS):
        reads[g].wait()
        part = jnp.dot(weight_ref[g], in_ref[:, group(g)], preferred_element_type=jnp.float32)
        out_ref[:, group(g)] = part[:tok_rows].astype(out_ref.dtype)
        total = total + part[tok_rows:]
    for i in range(EXTRA):
        out_ref[:, group(SLOTS + i)] = total[i * tok_rows : (i + 1) * tok_rows].astype(out_ref.dtype)


def combine(planned, returned, out_shape):
    slot, mix = planned
    given = pl.BlockSpec(memory_space=pl.ANY)
    return pl.pallas_call(
        combine_kernel,
        out_shape=out_shape,
        in_specs=[given, given, given],
        out_specs=pl.BlockSpec(memory_space=pltpu.VMEM),
        scratch_shapes=[
            pltpu.VMEM(slot.shape, slot.dtype),
            pltpu.VMEM(mix.shape, mix.dtype),
            pltpu.VMEM(returned.shape, returned.dtype),
            pltpu.VMEM((SLOTS, (1 + EXTRA) * out_shape.shape[0], slot.shape[1]), jnp.bfloat16),
            pltpu.SemaphoreType.DMA,
            pltpu.SemaphoreType.DMA,
            pltpu.SemaphoreType.DMA((SLOTS,)),
        ],
        compiler_params=pltpu.CompilerParams(vmem_limit_bytes=32 * MIB),
        name="combine",
    )(*(pltpu.with_memory_space_constraint(a, pltpu.HBM) for a in (slot, mix, returned)))


def exchange(blocks, experts):
    shape = blocks.shape
    moved = lax.all_to_all(
        blocks.reshape(experts, ROWS, shape[1]),
        ("expert", "helper"),
        split_axis=0,
        concat_axis=0,
        tiled=True,
    )
    return moved.reshape(shape)


def shards(tokens, expert_ids, gate_weights, w_gate_up, gu_scales, w_down, down_scales):
    experts = lax.axis_size("expert") * lax.axis_size("helper")
    hidden_width = w_down.shape[1]
    tile = 256
    arrived = exchange(pack(tokens, expert_ids, experts), experts)
    wide = tile // QBLK

    def place(j):
        part, block = divmod(j, hidden_width // QBLK)
        return block // wide * 2 * wide + part * wide + block % wide

    gate_up = dequant(w_gate_up[0], gu_scales[0], 256, place)
    down = dequant(w_down[0], down_scales[0], 128, lambda j: j)
    planned = plan(expert_ids, gate_weights, experts)
    returned = exchange(expert(arrived, gate_up, down, tile), experts)
    return combine(planned, returned, jax.ShapeDtypeStruct(tokens.shape, tokens.dtype))


def solution(mesh):
    rows = ("expert", "helper")
    placed = (P(rows, None),) * 3 + (P(rows, None, None),) * 4
    return jax.shard_map(
        shards, mesh=mesh, in_specs=placed, out_specs=P(rows, None), check_vma=False
    )
```

```python
import functools

import jax
import jax.numpy as jnp
from jax import lax
from jax.experimental import pallas as pl
from jax.experimental.pallas import tpu as pltpu
from jax.sharding import PartitionSpec as P

QBLK = 128
SLOTS = 5
ROWS = 8
EXTRA = ROWS - SLOTS
MIB = 1 << 20


def iota(shape, dim):
    return lax.broadcasted_iota(jnp.int32, shape, dim)


def slots_of(ids, experts):
    tok_rows, route_count = ids.shape
    expert_of = iota((tok_rows, experts), 1)
    hit = jnp.zeros((tok_rows, experts), jnp.float32)
    for k in range(route_count):
        hit = hit + jnp.where(ids[:, k : k + 1] == expert_of, 1.0, 0.0)
    earlier = jnp.where(iota((tok_rows, tok_rows), 0) > iota((tok_rows, tok_rows), 1), 1.0, 0.0)
    rank = jnp.dot(
        earlier.astype(jnp.bfloat16), hit.astype(jnp.bfloat16), preferred_element_type=jnp.float32
    )
    return jnp.where(hit > 0.5, rank, -1.0)


def slots_for(ids, experts):
    route_count, tok_rows = ids.shape
    expert_of = iota((experts, tok_rows), 0)
    hit = jnp.zeros((experts, tok_rows), jnp.float32)
    for k in range(route_count):
        hit = hit + jnp.where(ids[k : k + 1, :] == expert_of, 1.0, 0.0)
    earlier = jnp.where(iota((tok_rows, tok_rows), 0) < iota((tok_rows, tok_rows), 1), 1.0, 0.0)
    rank = jnp.dot(
        hit.astype(jnp.bfloat16), earlier.astype(jnp.bfloat16), preferred_element_type=jnp.float32
    )
    return jnp.where(hit > 0.5, rank, -1.0)


ALWAYS = 99.0
AHEAD = 3


def pack_kernel(
    ids_given_ref, given_ref, out_ref, ids_ref, tok_ref, block_ref, slot_ref, ids_sem, tok_sem, out_sem
):
    tok_rows, feat_width = tok_ref.shape
    group_width = feat_width // ROWS
    block_rows = block_ref.shape[0]
    experts = block_rows // ROWS
    parts = 1 + EXTRA
    fetch_ids = pltpu.make_async_copy(ids_given_ref, ids_ref, ids_sem)
    fetch_ids.start()
    fetch = pltpu.make_async_copy(given_ref, tok_ref, tok_sem)
    fetch.start()
    fetch_ids.wait()

    slot = slots_for(ids_ref[...], experts).astype(jnp.bfloat16)
    repeat = jnp.where(
        iota((block_rows, experts), 0) // ROWS == iota((block_rows, experts), 1), 1.0, 0.0
    ).astype(jnp.bfloat16)
    spread = jnp.dot(
        repeat, jnp.concatenate([slot] * parts, axis=1), preferred_element_type=jnp.float32
    )
    shape = (block_rows, parts * tok_rows)
    row = iota(shape, 0) % ROWS
    part = iota(shape, 1) // tok_rows
    own = (part == 0) & (row.astype(jnp.float32) == spread) & (row < SLOTS)
    shared = (part > 0) & (row == SLOTS - 1 + part)
    slot_ref[...] = jnp.where(own, ALWAYS, jnp.where(shared, spread, -1.0))
    fetch.wait()

    def group(g):
        return slice(g * group_width, (g + 1) * group_width)

    writes = []
    for g in range(SLOTS):
        code = slot_ref[...]
        chosen = jnp.where((code == ALWAYS) | (code == float(g)), 1.0, 0.0).astype(jnp.bfloat16)
        source = jnp.concatenate(
            [tok_ref[:, group(f)] for f in (g, *range(SLOTS, ROWS))], axis=0
        )
        block_ref[:, group(g)] = jnp.dot(
            chosen, source, preferred_element_type=jnp.float32
        ).astype(block_ref.dtype)
        writes.append(
            pltpu.make_async_copy(block_ref.at[:, group(g)], out_ref.at[:, group(g)], out_sem.at[g])
        )
        writes[-1].start()
    for write in writes:
        write.wait()


def pack(tokens, expert_ids, experts):
    tok_rows, feat_width = tokens.shape
    shape = (experts * ROWS, feat_width // ROWS * SLOTS)
    return pl.pallas_call(
        pack_kernel,
        out_shape=pltpu.HBM(shape, tokens.dtype),
        in_specs=[pl.BlockSpec(memory_space=pl.ANY)] * 2,
        out_specs=pl.BlockSpec(memory_space=pl.ANY),
        scratch_shapes=[
            pltpu.VMEM(expert_ids.shape[::-1], expert_ids.dtype),
            pltpu.VMEM(tokens.shape, tokens.dtype),
            pltpu.VMEM(shape, tokens.dtype),
            pltpu.VMEM((shape[0], (1 + EXTRA) * tok_rows), jnp.float32),
            pltpu.SemaphoreType.DMA,
            pltpu.SemaphoreType.DMA,
            pltpu.SemaphoreType.DMA((SLOTS,)),
        ],
        compiler_params=pltpu.CompilerParams(vmem_limit_bytes=32 * MIB),
        name="pack",
    )(*(pltpu.with_memory_space_constraint(a, pltpu.HBM) for a in (expert_ids.T, tokens)))


def plan_kernel(ids_ref, gate_ref, slot_ref, mix_ref):
    tok_rows, route_count = ids_ref.shape
    block_rows = slot_ref.shape[1]
    experts = block_rows // ROWS
    gates = gate_ref[...]
    mix = gates / jnp.sum(gates, axis=1, keepdims=True)
    slot = slots_of(ids_ref[...], experts)
    expert_of = iota((tok_rows, experts), 1)
    mix_of = jnp.zeros((tok_rows, experts), jnp.float32)
    for k in range(route_count):
        mix_of = mix_of + jnp.where(ids_ref[:, k : k + 1] == expert_of, mix[:, k : k + 1], 0.0)
    repeat = jnp.where(
        iota((experts, block_rows), 1) // ROWS == iota((experts, block_rows), 0), 1.0, 0.0
    ).astype(jnp.bfloat16)
    slot_ref[...] = jnp.dot(slot.astype(jnp.bfloat16), repeat, preferred_element_type=jnp.float32)
    mix_ref[...] = jnp.dot(
        mix_of.astype(jnp.bfloat16), repeat, preferred_element_type=jnp.float32
    )


def plan(expert_ids, gate_weights, experts):
    shape = (expert_ids.shape[0], experts * ROWS)
    return pl.pallas_call(
        plan_kernel,
        out_shape=(pltpu.HBM(shape, jnp.float32), pltpu.HBM(shape, jnp.float32)),
        compiler_params=pltpu.CompilerParams(vmem_limit_bytes=16 * MIB),
        cost_estimate=pl.CostEstimate(flops=10**8, bytes_accessed=10**6, transcendentals=0),
        name="plan",
    )(expert_ids, gate_weights)


def dequant_kernel(place, scale_ref, weight_ref, out_ref):
    row_blocks, col_blocks = (n // QBLK for n in weight_ref.shape)
    step = pl.program_id(0)
    for i in range(row_blocks):
        rows = slice(i * QBLK, (i + 1) * QBLK)
        for j in range(col_blocks):
            scale = scale_ref[step * row_blocks + i, j]
            scaled = weight_ref[rows, j * QBLK : (j + 1) * QBLK].astype(jnp.float32) * scale
            out_ref[rows, place(j) * QBLK : (place(j) + 1) * QBLK] = scaled.astype(out_ref.dtype)


def dequant(weight, scales, rows, place):
    row_count, col_count = weight.shape
    block = pl.BlockSpec((rows, col_count), lambda i: (i, 0))
    return pl.pallas_call(
        functools.partial(dequant_kernel, place),
        grid=(row_count // rows,),
        out_shape=pltpu.HBM(weight.shape, weight.dtype),
        in_specs=[pl.BlockSpec(memory_space=pltpu.SMEM), block],
        out_specs=block,
        compiler_params=pltpu.CompilerParams(vmem_limit_bytes=16 * MIB),
        cost_estimate=pl.CostEstimate(
            flops=row_count * col_count, bytes_accessed=4 * row_count * col_count, transcendentals=0
        ),
        name="dequant",
    )(scales, pltpu.with_memory_space_constraint(weight, pltpu.HBM))


def expert_kernel(
    hidden_tile, given_ref, gu_given_ref, down_given_ref, out_ref,
    in_ref, gu_ref, down_ref, x_ref, hidden_ref, result_ref, in_sem, gu_sem, down_sem, out_sem,
):
    group_width = result_ref.shape[2]
    runs, tiles = in_sem.shape[0], gu_sem.shape[0]
    span = in_ref.shape[0] // runs
    sources = span // ROWS
    kept = sources * SLOTS
    order = (*range(SLOTS - 1, ROWS), *range(SLOTS - 1))

    def group(g):
        return slice(g * group_width, (g + 1) * group_width)

    def run_rows(run, rows):
        return slice(run * rows, (run + 1) * rows)

    def copies(given, held, sem, places):
        return [
            pltpu.make_async_copy(given.at[p], held.at[p], sem.at[i]) for i, p in enumerate(places)
        ]

    in_copies = copies(given_ref, in_ref, in_sem, [(run_rows(r, span),) for r in range(runs)])
    gu_places = [(slice(None), run_rows(t, 2 * hidden_tile)) for t in range(tiles)]
    gu_copies = copies(gu_given_ref, gu_ref, gu_sem, gu_places)
    down_copies = copies(down_given_ref, down_ref, down_sem, [(slice(None), group(f)) for f in order])
    out_copies = [
        pltpu.make_async_copy(result_ref.at[g], out_ref.at[:, group(g)], out_sem.at[g])
        for g in range(SLOTS)
    ]

    def turned(back):
        to, come = iota((span, span), 1 if back else 0), iota((span, span), 0 if back else 1)
        same = (to // sources == come % ROWS) & (to % sources == come // ROWS)
        return jnp.where(same, 1.0, 0.0).astype(jnp.bfloat16)

    for copy in in_copies + gu_copies[:1]:
        copy.start()
    unpack = turned(False)
    for run in range(runs):
        in_copies[run].wait()
        for g in range(SLOTS):
            moved = jnp.dot(
                unpack, in_ref[run_rows(run, span), group(g)], preferred_element_type=jnp.float32
            ).astype(x_ref.dtype)
            for row in range(ROWS):
                slot, feature = (row, g) if row < SLOTS else (g, row)
                first = run * kept + slot * sources
                x_ref[first : first + sources, group(feature)] = moved[run_rows(row, sources)]
    for tile in range(tiles):
        gu_copies[tile].wait()
        for copy in gu_copies[tile + 1 : tile + 2] + down_copies[
            tile * ROWS // tiles : (tile + 1) * ROWS // tiles
        ]:
            copy.start()
        pre = jnp.dot(x_ref[...], gu_ref[gu_places[tile]], preferred_element_type=jnp.float32)
        gate, up = pre[:, :hidden_tile], pre[:, hidden_tile:]
        hidden_ref[:, run_rows(tile, hidden_tile)] = (gate / (1.0 + jnp.exp(-gate)) * up).astype(
            hidden_ref.dtype
        )
    pack_again = turned(True)

    def product(first, count):
        cols = slice(first * group_width, (first + count) * group_width)
        return jnp.dot(
            hidden_ref[...], down_ref[:, cols], preferred_element_type=jnp.float32
        ).astype(x_ref.dtype)

    def give(feature, result):
        for run in range(runs):
            first = run * kept + feature * sources
            gathered = jnp.concatenate(
                [result[run_rows(run, kept)]]
                + [x_ref[first : first + sources, group(f)] for f in range(SLOTS, ROWS)],
                axis=0,
            )
            result_ref[feature, run_rows(run, span), :] = jnp.dot(
                pack_again, gathered, preferred_element_type=jnp.float32
            ).astype(result_ref.dtype)
        out_copies[feature].start()

    for copy in down_copies[:EXTRA + 1]:
        copy.wait()
    result = product(SLOTS - 1, EXTRA + 1)
    x_ref[:, SLOTS * group_width :] = result[:, group_width:]
    give(SLOTS - 1, result[:, :group_width])
    for copy in down_copies[EXTRA + 1 :]:
        copy.wait()
    for feature in range(0, SLOTS - 1, 2):
        result = product(feature, 2)
        give(feature, result[:, :group_width])
        give(feature + 1, result[:, group_width:])
    for copy in out_copies:
        copy.wait()


def expert(arrived, gate_up, down, hidden_tile):
    block_rows, packed_width = arrived.shape
    feat_width, hidden_width = gate_up.shape[0], down.shape[0]
    group_width = feat_width // ROWS
    live_rows = block_rows // ROWS * SLOTS
    runs = block_rows // 256
    tiles = hidden_width // hidden_tile
    given = pl.BlockSpec(memory_space=pl.ANY)

    return pl.pallas_call(
        functools.partial(expert_kernel, hidden_tile),
        out_shape=pltpu.HBM(arrived.shape, arrived.dtype),
        in_specs=[given, given, given],
        out_specs=given,
        scratch_shapes=[
            pltpu.VMEM(arrived.shape, jnp.bfloat16),
            pltpu.VMEM(gate_up.shape, jnp.bfloat16),
            pltpu.VMEM(down.shape, jnp.bfloat16),
            pltpu.VMEM((live_rows, feat_width), jnp.bfloat16),
            pltpu.VMEM((live_rows, hidden_width), jnp.bfloat16),
            pltpu.VMEM((SLOTS, block_rows, group_width), jnp.bfloat16),
            pltpu.SemaphoreType.DMA((runs,)),
            pltpu.SemaphoreType.DMA((tiles,)),
            pltpu.SemaphoreType.DMA((ROWS,)),
            pltpu.SemaphoreType.DMA((SLOTS,)),
        ],
        compiler_params=pltpu.CompilerParams(vmem_limit_bytes=56 * MIB),
        cost_estimate=pl.CostEstimate(
            flops=2 * live_rows * 3 * feat_width * hidden_width,
            bytes_accessed=6 * feat_width * hidden_width + 4 * block_rows * packed_width,
            transcendentals=live_rows * hidden_width,
        ),
        name="expert",
    )(*(pltpu.with_memory_space_constraint(a, pltpu.HBM) for a in (arrived, gate_up, down)))


def combine_kernel(
    slot_given_ref, mix_given_ref, given_ref, out_ref,
    slot_ref, mix_ref, in_ref, weight_ref, slot_sem, mix_sem, in_sem,
):
    tok_rows, feat_width = out_ref.shape
    group_width = feat_width // ROWS

    def group(g):
        return slice(g * group_width, (g + 1) * group_width)

    plans = [
        pltpu.make_async_copy(slot_given_ref, slot_ref, slot_sem),
        pltpu.make_async_copy(mix_given_ref, mix_ref, mix_sem),
    ]
    reads = [
        pltpu.make_async_copy(given_ref.at[:, group(g)], in_ref.at[:, group(g)], in_sem.at[g])
        for g in range(SLOTS)
    ]
    for copy in plans + reads[:AHEAD]:
        copy.start()
    for copy in plans:
        copy.wait()
    slot, mix = slot_ref[...], mix_ref[...]
    row = iota(slot.shape, 1) % ROWS
    own = jnp.where((row < SLOTS) & (slot == row.astype(jnp.float32)), mix, 0.0)
    own = own.astype(weight_ref.dtype)
    for g in range(SLOTS):
        weight_ref[g, :tok_rows] = own
        here = jnp.where(slot == float(g), mix, 0.0)
        for i in range(EXTRA):
            weight_ref[g, (1 + i) * tok_rows : (2 + i) * tok_rows] = jnp.where(
                row == SLOTS + i, here, 0.0
            ).astype(weight_ref.dtype)
    total = jnp.zeros((EXTRA * tok_rows, group_width), jnp.float32)
    for g in range(SLOTS):
        reads[g].wait()
        for copy in reads[g + AHEAD : g + AHEAD + 1]:
            copy.start()
        part = jnp.dot(weight_ref[g], in_ref[:, group(g)], preferred_element_type=jnp.float32)
        out_ref[:, group(g)] = part[:tok_rows].astype(out_ref.dtype)
        total = total + part[tok_rows:]
    for i in range(EXTRA):
        out_ref[:, group(SLOTS + i)] = total[i * tok_rows : (i + 1) * tok_rows].astype(out_ref.dtype)


def combine(planned, returned, out_shape):
    slot, mix = planned
    given = pl.BlockSpec(memory_space=pl.ANY)
    return pl.pallas_call(
        combine_kernel,
        out_shape=out_shape,
        in_specs=[given, given, given],
        out_specs=pl.BlockSpec(memory_space=pltpu.VMEM),
        scratch_shapes=[
            pltpu.VMEM(slot.shape, slot.dtype),
            pltpu.VMEM(mix.shape, mix.dtype),
            pltpu.VMEM(returned.shape, returned.dtype),
            pltpu.VMEM((SLOTS, (1 + EXTRA) * out_shape.shape[0], slot.shape[1]), jnp.bfloat16),
            pltpu.SemaphoreType.DMA,
            pltpu.SemaphoreType.DMA,
            pltpu.SemaphoreType.DMA((SLOTS,)),
        ],
        compiler_params=pltpu.CompilerParams(vmem_limit_bytes=32 * MIB),
        name="combine",
    )(*(pltpu.with_memory_space_constraint(a, pltpu.HBM) for a in (slot, mix, returned)))


def exchange(blocks, experts):
    shape = blocks.shape
    moved = lax.all_to_all(
        blocks.reshape(experts, ROWS, shape[1]),
        ("expert", "helper"),
        split_axis=0,
        concat_axis=0,
        tiled=True,
    )
    return moved.reshape(shape)


def shards(tokens, expert_ids, gate_weights, w_gate_up, gu_scales, w_down, down_scales):
    experts = lax.axis_size("expert") * lax.axis_size("helper")
    hidden_width = w_down.shape[1]
    tile = 256
    arrived = exchange(pack(tokens, expert_ids, experts), experts)
    wide = tile // QBLK

    def place(j):
        part, block = divmod(j, hidden_width // QBLK)
        return block // wide * 2 * wide + part * wide + block % wide

    gate_up = dequant(w_gate_up[0], gu_scales[0], 256, place)
    down = dequant(w_down[0], down_scales[0], 128, lambda j: j)
    planned = plan(expert_ids, gate_weights, experts)
    returned = exchange(expert(arrived, gate_up, down, tile), experts)
    return combine(planned, returned, jax.ShapeDtypeStruct(tokens.shape, tokens.dtype))


def solution(mesh):
    rows = ("expert", "helper")
    placed = (P(rows, None),) * 3 + (P(rows, None, None),) * 4
    return jax.shard_map(
        shards, mesh=mesh, in_specs=placed, out_specs=P(rows, None), check_vma=False
    )
```

```python
import functools

import jax
import jax.numpy as jnp
from jax import lax
from jax.experimental import pallas as pl
from jax.experimental.pallas import tpu as pltpu
from jax.sharding import PartitionSpec as P

QBLK = 128
SLOTS = 5
ROWS = 8
EXTRA = ROWS - SLOTS
MIB = 1 << 20


def iota(shape, dim):
    return lax.broadcasted_iota(jnp.int32, shape, dim)


def slots_of(ids, experts):
    tok_rows, route_count = ids.shape
    expert_of = iota((tok_rows, experts), 1)
    hit = jnp.zeros((tok_rows, experts), jnp.float32)
    for k in range(route_count):
        hit = hit + jnp.where(ids[:, k : k + 1] == expert_of, 1.0, 0.0)
    earlier = jnp.where(iota((tok_rows, tok_rows), 0) > iota((tok_rows, tok_rows), 1), 1.0, 0.0)
    rank = jnp.dot(
        earlier.astype(jnp.bfloat16), hit.astype(jnp.bfloat16), preferred_element_type=jnp.float32
    )
    return jnp.where(hit > 0.5, rank, -1.0)


def slots_for(ids, experts):
    route_count, tok_rows = ids.shape
    expert_of = iota((experts, tok_rows), 0)
    hit = jnp.zeros((experts, tok_rows), jnp.float32)
    for k in range(route_count):
        hit = hit + jnp.where(ids[k : k + 1, :] == expert_of, 1.0, 0.0)
    earlier = jnp.where(iota((tok_rows, tok_rows), 0) < iota((tok_rows, tok_rows), 1), 1.0, 0.0)
    rank = jnp.dot(
        hit.astype(jnp.bfloat16), earlier.astype(jnp.bfloat16), preferred_element_type=jnp.float32
    )
    return jnp.where(hit > 0.5, rank, -1.0)


ALWAYS = 99.0


def pack_kernel(
    ids_given_ref, given_ref, out_ref, ids_ref, tok_ref, block_ref, slot_ref, ids_sem, tok_sem, out_sem
):
    tok_rows, feat_width = tok_ref.shape
    group_width = feat_width // ROWS
    block_rows = block_ref.shape[0]
    experts = block_rows // ROWS
    parts = 1 + EXTRA
    fetch_ids = pltpu.make_async_copy(ids_given_ref, ids_ref, ids_sem)
    fetch_ids.start()
    fetch = pltpu.make_async_copy(given_ref, tok_ref, tok_sem)
    fetch.start()
    fetch_ids.wait()

    slot = slots_for(ids_ref[...], experts).astype(jnp.bfloat16)
    repeat = jnp.where(
        iota((block_rows, experts), 0) // ROWS == iota((block_rows, experts), 1), 1.0, 0.0
    ).astype(jnp.bfloat16)
    spread = jnp.dot(
        repeat, jnp.concatenate([slot] * parts, axis=1), preferred_element_type=jnp.float32
    )
    shape = (block_rows, parts * tok_rows)
    row = iota(shape, 0) % ROWS
    part = iota(shape, 1) // tok_rows
    own = (part == 0) & (row.astype(jnp.float32) == spread) & (row < SLOTS)
    shared = (part > 0) & (row == SLOTS - 1 + part)
    slot_ref[...] = jnp.where(own, ALWAYS, jnp.where(shared, spread, -1.0))
    fetch.wait()

    def group(g):
        return slice(g * group_width, (g + 1) * group_width)

    writes = []
    for g in range(SLOTS):
        code = slot_ref[...]
        chosen = jnp.where((code == ALWAYS) | (code == float(g)), 1.0, 0.0).astype(jnp.bfloat16)
        source = jnp.concatenate(
            [tok_ref[:, group(f)] for f in (g, *range(SLOTS, ROWS))], axis=0
        )
        block_ref[:, group(g)] = jnp.dot(
            chosen, source, preferred_element_type=jnp.float32
        ).astype(block_ref.dtype)
        writes.append(
            pltpu.make_async_copy(block_ref.at[:, group(g)], out_ref.at[:, group(g)], out_sem.at[g])
        )
        writes[-1].start()
    for write in writes:
        write.wait()


def pack(tokens, expert_ids, experts):
    tok_rows, feat_width = tokens.shape
    shape = (experts * ROWS, feat_width // ROWS * SLOTS)
    return pl.pallas_call(
        pack_kernel,
        out_shape=pltpu.HBM(shape, tokens.dtype),
        in_specs=[pl.BlockSpec(memory_space=pl.ANY)] * 2,
        out_specs=pl.BlockSpec(memory_space=pl.ANY),
        scratch_shapes=[
            pltpu.VMEM(expert_ids.shape[::-1], expert_ids.dtype),
            pltpu.VMEM(tokens.shape, tokens.dtype),
            pltpu.VMEM(shape, tokens.dtype),
            pltpu.VMEM((shape[0], (1 + EXTRA) * tok_rows), jnp.float32),
            pltpu.SemaphoreType.DMA,
            pltpu.SemaphoreType.DMA,
            pltpu.SemaphoreType.DMA((SLOTS,)),
        ],
        compiler_params=pltpu.CompilerParams(vmem_limit_bytes=32 * MIB),
        name="pack",
    )(*(pltpu.with_memory_space_constraint(a, pltpu.HBM) for a in (expert_ids.T, tokens)))


def plan_kernel(ids_ref, gate_ref, weight_ref):
    tok_rows, route_count = ids_ref.shape
    block_rows = weight_ref.shape[2]
    experts = block_rows // ROWS
    gates = gate_ref[...]
    mix = gates / jnp.sum(gates, axis=1, keepdims=True)
    slot = slots_of(ids_ref[...], experts)
    expert_of = iota((tok_rows, experts), 1)
    mix_of = jnp.zeros((tok_rows, experts), jnp.float32)
    for k in range(route_count):
        mix_of = mix_of + jnp.where(ids_ref[:, k : k + 1] == expert_of, mix[:, k : k + 1], 0.0)
    repeat = jnp.where(
        iota((experts, block_rows), 1) // ROWS == iota((experts, block_rows), 0), 1.0, 0.0
    ).astype(jnp.bfloat16)
    slot = jnp.dot(slot.astype(jnp.bfloat16), repeat, preferred_element_type=jnp.float32)
    mix = jnp.dot(mix_of.astype(jnp.bfloat16), repeat, preferred_element_type=jnp.float32)
    row = iota(slot.shape, 1) % ROWS
    own = jnp.where((row < SLOTS) & (slot == row.astype(jnp.float32)), mix, 0.0)
    own = own.astype(weight_ref.dtype)
    for g in range(SLOTS):
        weight_ref[g, :tok_rows] = own
        here = jnp.where(slot == float(g), mix, 0.0)
        for i in range(EXTRA):
            weight_ref[g, (1 + i) * tok_rows : (2 + i) * tok_rows] = jnp.where(
                row == SLOTS + i, here, 0.0
            ).astype(weight_ref.dtype)


def plan(expert_ids, gate_weights, experts):
    shape = (SLOTS, (1 + EXTRA) * expert_ids.shape[0], experts * ROWS)
    return pl.pallas_call(
        plan_kernel,
        out_shape=pltpu.HBM(shape, jnp.bfloat16),
        compiler_params=pltpu.CompilerParams(vmem_limit_bytes=16 * MIB),
        cost_estimate=pl.CostEstimate(flops=10**8, bytes_accessed=10**6, transcendentals=0),
        name="plan",
    )(expert_ids, gate_weights)


def dequant_kernel(place, scale_ref, weight_ref, out_ref):
    row_blocks, col_blocks = (n // QBLK for n in weight_ref.shape)
    step = pl.program_id(0)
    for i in range(row_blocks):
        rows = slice(i * QBLK, (i + 1) * QBLK)
        for j in range(col_blocks):
            scale = scale_ref[step * row_blocks + i, j]
            scaled = weight_ref[rows, j * QBLK : (j + 1) * QBLK].astype(jnp.float32) * scale
            out_ref[rows, place(j) * QBLK : (place(j) + 1) * QBLK] = scaled.astype(out_ref.dtype)


def dequant(weight, scales, rows, place):
    row_count, col_count = weight.shape
    block = pl.BlockSpec((rows, col_count), lambda i: (i, 0))
    return pl.pallas_call(
        functools.partial(dequant_kernel, place),
        grid=(row_count // rows,),
        out_shape=pltpu.HBM(weight.shape, weight.dtype),
        in_specs=[pl.BlockSpec(memory_space=pltpu.SMEM), block],
        out_specs=block,
        compiler_params=pltpu.CompilerParams(vmem_limit_bytes=16 * MIB),
        cost_estimate=pl.CostEstimate(
            flops=row_count * col_count, bytes_accessed=4 * row_count * col_count, transcendentals=0
        ),
        name="dequant",
    )(scales, pltpu.with_memory_space_constraint(weight, pltpu.HBM))


def expert_kernel(
    hidden_tile, given_ref, gu_given_ref, down_given_ref, out_ref,
    in_ref, gu_ref, down_ref, x_ref, hidden_ref, in_sem, gu_sem, down_sem,
):
    group_width = x_ref.shape[1] // ROWS
    runs, tiles = in_sem.shape[0], gu_sem.shape[0]
    span = in_ref.shape[0] // runs
    sources = span // ROWS
    kept = sources * SLOTS
    order = (*range(SLOTS - 1, ROWS), *range(SLOTS - 1))

    def group(g):
        return slice(g * group_width, (g + 1) * group_width)

    def run_rows(run, rows):
        return slice(run * rows, (run + 1) * rows)

    def copies(given, held, sem, places):
        return [
            pltpu.make_async_copy(given.at[p], held.at[p], sem.at[i]) for i, p in enumerate(places)
        ]

    in_copies = copies(given_ref, in_ref, in_sem, [(run_rows(r, span),) for r in range(runs)])
    gu_places = [(slice(None), run_rows(t, 2 * hidden_tile)) for t in range(tiles)]
    gu_copies = copies(gu_given_ref, gu_ref, gu_sem, gu_places)
    down_copies = copies(down_given_ref, down_ref, down_sem, [(slice(None), group(f)) for f in order])

    def turned(back):
        to, come = iota((span, span), 1 if back else 0), iota((span, span), 0 if back else 1)
        same = (to // sources == come % ROWS) & (to % sources == come // ROWS)
        return jnp.where(same, 1.0, 0.0).astype(jnp.bfloat16)

    for copy in in_copies + gu_copies[:1]:
        copy.start()
    unpack = turned(False)
    for run in range(runs):
        in_copies[run].wait()
        for g in range(SLOTS):
            moved = jnp.dot(
                unpack, in_ref[run_rows(run, span), group(g)], preferred_element_type=jnp.float32
            ).astype(x_ref.dtype)
            for row in range(ROWS):
                slot, feature = (row, g) if row < SLOTS else (g, row)
                first = run * kept + slot * sources
                x_ref[first : first + sources, group(feature)] = moved[run_rows(row, sources)]
    for tile in range(tiles):
        gu_copies[tile].wait()
        for copy in gu_copies[tile + 1 : tile + 2] + down_copies[
            tile * ROWS // tiles : (tile + 1) * ROWS // tiles
        ]:
            copy.start()
        pre = jnp.dot(x_ref[...], gu_ref[gu_places[tile]], preferred_element_type=jnp.float32)
        gate, up = pre[:, :hidden_tile], pre[:, hidden_tile:]
        hidden_ref[:, run_rows(tile, hidden_tile)] = (gate / (1.0 + jnp.exp(-gate)) * up).astype(
            hidden_ref.dtype
        )
    pack_again = turned(True)

    def product(first, count):
        cols = slice(first * group_width, (first + count) * group_width)
        return jnp.dot(
            hidden_ref[...], down_ref[:, cols], preferred_element_type=jnp.float32
        ).astype(x_ref.dtype)

    def give(feature, result):
        for run in range(runs):
            first = run * kept + feature * sources
            gathered = jnp.concatenate(
                [result[run_rows(run, kept)]]
                + [x_ref[first : first + sources, group(f)] for f in range(SLOTS, ROWS)],
                axis=0,
            )
            out_ref[run_rows(run, span), group(feature)] = jnp.dot(
                pack_again, gathered, preferred_element_type=jnp.float32
            ).astype(out_ref.dtype)

    for copy in down_copies[:EXTRA + 1]:
        copy.wait()
    result = product(SLOTS - 1, EXTRA + 1)
    x_ref[:, SLOTS * group_width :] = result[:, group_width:]
    give(SLOTS - 1, result[:, :group_width])
    for copy in down_copies[EXTRA + 1 :]:
        copy.wait()
    for feature in range(0, SLOTS - 1, 2):
        result = product(feature, 2)
        give(feature, result[:, :group_width])
        give(feature + 1, result[:, group_width:])


def expert(arrived, gate_up, down, hidden_tile):
    block_rows, packed_width = arrived.shape
    feat_width, hidden_width = gate_up.shape[0], down.shape[0]
    live_rows = block_rows // ROWS * SLOTS
    runs = block_rows // 256
    tiles = hidden_width // hidden_tile
    given = pl.BlockSpec(memory_space=pl.ANY)

    return pl.pallas_call(
        functools.partial(expert_kernel, hidden_tile),
        out_shape=pltpu.VMEM(arrived.shape, arrived.dtype),
        in_specs=[given, given, given],
        out_specs=pl.BlockSpec(memory_space=pltpu.VMEM),
        scratch_shapes=[
            pltpu.VMEM(arrived.shape, jnp.bfloat16),
            pltpu.VMEM(gate_up.shape, jnp.bfloat16),
            pltpu.VMEM(down.shape, jnp.bfloat16),
            pltpu.VMEM((live_rows, feat_width), jnp.bfloat16),
            pltpu.VMEM((live_rows, hidden_width), jnp.bfloat16),
            pltpu.SemaphoreType.DMA((runs,)),
            pltpu.SemaphoreType.DMA((tiles,)),
            pltpu.SemaphoreType.DMA((ROWS,)),
        ],
        compiler_params=pltpu.CompilerParams(vmem_limit_bytes=48 * MIB),
        cost_estimate=pl.CostEstimate(
            flops=2 * live_rows * 3 * feat_width * hidden_width,
            bytes_accessed=6 * feat_width * hidden_width + 4 * block_rows * packed_width,
            transcendentals=live_rows * hidden_width,
        ),
        name="expert",
    )(*(pltpu.with_memory_space_constraint(a, pltpu.HBM) for a in (arrived, gate_up, down)))


def combine_kernel(weight_ref, in_ref, out_ref):
    tok_rows, feat_width = out_ref.shape
    group_width = feat_width // ROWS

    def group(g):
        return slice(g * group_width, (g + 1) * group_width)

    total = jnp.zeros((EXTRA * tok_rows, group_width), jnp.float32)
    for g in range(SLOTS):
        part = jnp.dot(weight_ref[g], in_ref[:, group(g)], preferred_element_type=jnp.float32)
        out_ref[:, group(g)] = part[:tok_rows].astype(out_ref.dtype)
        total = total + part[tok_rows:]
    for i in range(EXTRA):
        out_ref[:, group(SLOTS + i)] = total[i * tok_rows : (i + 1) * tok_rows].astype(out_ref.dtype)


def combine(weights, returned, out_shape):
    held = pl.BlockSpec(memory_space=pltpu.VMEM)
    return pl.pallas_call(
        combine_kernel,
        out_shape=out_shape,
        in_specs=[held, held],
        out_specs=held,
        compiler_params=pltpu.CompilerParams(vmem_limit_bytes=24 * MIB),
        name="combine",
    )(*(pltpu.with_memory_space_constraint(a, pltpu.VMEM) for a in (weights, returned)))


def exchange(blocks, experts):
    shape = blocks.shape
    moved = lax.all_to_all(
        blocks.reshape(experts, ROWS, shape[1]),
        ("expert", "helper"),
        split_axis=0,
        concat_axis=0,
        tiled=True,
    )
    return moved.reshape(shape)


def shards(tokens, expert_ids, gate_weights, w_gate_up, gu_scales, w_down, down_scales):
    experts = lax.axis_size("expert") * lax.axis_size("helper")
    hidden_width = w_down.shape[1]
    tile = 256
    arrived = exchange(pack(tokens, expert_ids, experts), experts)
    wide = tile // QBLK

    def place(j):
        part, block = divmod(j, hidden_width // QBLK)
        return block // wide * 2 * wide + part * wide + block % wide

    gate_up = dequant(w_gate_up[0], gu_scales[0], 256, place)
    down = dequant(w_down[0], down_scales[0], 128, lambda j: j)
    planned = plan(expert_ids, gate_weights, experts)
    arrived, planned = lax.optimization_barrier((arrived, planned))
    returned = exchange(expert(arrived, gate_up, down, tile), experts)
    return combine(planned, returned, jax.ShapeDtypeStruct(tokens.shape, tokens.dtype))


def solution(mesh):
    rows = ("expert", "helper")
    placed = (P(rows, None),) * 3 + (P(rows, None, None),) * 4
    return jax.shard_map(
        shards, mesh=mesh, in_specs=placed, out_specs=P(rows, None), check_vma=False
    )
```

```python
import functools

import jax
import jax.numpy as jnp
from jax import lax
from jax.experimental import pallas as pl
from jax.experimental.pallas import tpu as pltpu
from jax.sharding import PartitionSpec as P

QBLK = 128
SLOTS = 5
ROWS = 8
EXTRA = ROWS - SLOTS
MIB = 1 << 20


def iota(shape, dim):
    return lax.broadcasted_iota(jnp.int32, shape, dim)


def slots_of(ids, experts):
    tok_rows, route_count = ids.shape
    expert_of = iota((tok_rows, experts), 1)
    hit = jnp.zeros((tok_rows, experts), jnp.float32)
    for k in range(route_count):
        hit = hit + jnp.where(ids[:, k : k + 1] == expert_of, 1.0, 0.0)
    earlier = jnp.where(iota((tok_rows, tok_rows), 0) > iota((tok_rows, tok_rows), 1), 1.0, 0.0)
    rank = jnp.dot(
        earlier.astype(jnp.bfloat16), hit.astype(jnp.bfloat16), preferred_element_type=jnp.float32
    )
    return jnp.where(hit > 0.5, rank, -1.0)


def slots_for(ids, experts):
    route_count, tok_rows = ids.shape
    expert_of = iota((experts, tok_rows), 0)
    hit = jnp.zeros((experts, tok_rows), jnp.float32)
    for k in range(route_count):
        hit = hit + jnp.where(ids[k : k + 1, :] == expert_of, 1.0, 0.0)
    earlier = jnp.where(iota((tok_rows, tok_rows), 0) < iota((tok_rows, tok_rows), 1), 1.0, 0.0)
    rank = jnp.dot(
        hit.astype(jnp.bfloat16), earlier.astype(jnp.bfloat16), preferred_element_type=jnp.float32
    )
    return jnp.where(hit > 0.5, rank, -1.0)


ALWAYS = 99.0


def pack_kernel(
    ids_given_ref, given_ref, out_ref, ids_ref, tok_ref, block_ref, slot_ref, ids_sem, tok_sem, out_sem
):
    tok_rows, feat_width = tok_ref.shape
    group_width = feat_width // ROWS
    block_rows = block_ref.shape[0]
    experts = block_rows // ROWS
    parts = 1 + EXTRA
    fetch_ids = pltpu.make_async_copy(ids_given_ref, ids_ref, ids_sem)
    fetch_ids.start()
    fetch = pltpu.make_async_copy(given_ref, tok_ref, tok_sem)
    fetch.start()
    fetch_ids.wait()

    slot = slots_for(ids_ref[...], experts).astype(jnp.bfloat16)
    repeat = jnp.where(
        iota((block_rows, experts), 0) // ROWS == iota((block_rows, experts), 1), 1.0, 0.0
    ).astype(jnp.bfloat16)
    spread = jnp.dot(
        repeat, jnp.concatenate([slot] * parts, axis=1), preferred_element_type=jnp.float32
    )
    shape = (block_rows, parts * tok_rows)
    row = iota(shape, 0) % ROWS
    part = iota(shape, 1) // tok_rows
    own = (part == 0) & (row.astype(jnp.float32) == spread) & (row < SLOTS)
    shared = (part > 0) & (row == SLOTS - 1 + part)
    slot_ref[...] = jnp.where(own, ALWAYS, jnp.where(shared, spread, -1.0))
    fetch.wait()

    def group(g):
        return slice(g * group_width, (g + 1) * group_width)

    writes = []
    for g in range(SLOTS):
        code = slot_ref[...]
        chosen = jnp.where((code == ALWAYS) | (code == float(g)), 1.0, 0.0).astype(jnp.bfloat16)
        source = jnp.concatenate(
            [tok_ref[:, group(f)] for f in (g, *range(SLOTS, ROWS))], axis=0
        )
        block_ref[:, group(g)] = jnp.dot(
            chosen, source, preferred_element_type=jnp.float32
        ).astype(block_ref.dtype)
        writes.append(
            pltpu.make_async_copy(block_ref.at[:, group(g)], out_ref.at[:, group(g)], out_sem.at[g])
        )
        writes[-1].start()
    for write in writes:
        write.wait()


def pack(tokens, expert_ids, experts):
    tok_rows, feat_width = tokens.shape
    shape = (experts * ROWS, feat_width // ROWS * SLOTS)
    return pl.pallas_call(
        pack_kernel,
        out_shape=pltpu.HBM(shape, tokens.dtype),
        in_specs=[pl.BlockSpec(memory_space=pl.ANY)] * 2,
        out_specs=pl.BlockSpec(memory_space=pl.ANY),
        scratch_shapes=[
            pltpu.VMEM(expert_ids.shape[::-1], expert_ids.dtype),
            pltpu.VMEM(tokens.shape, tokens.dtype),
            pltpu.VMEM(shape, tokens.dtype),
            pltpu.VMEM((shape[0], (1 + EXTRA) * tok_rows), jnp.float32),
            pltpu.SemaphoreType.DMA,
            pltpu.SemaphoreType.DMA,
            pltpu.SemaphoreType.DMA((SLOTS,)),
        ],
        compiler_params=pltpu.CompilerParams(vmem_limit_bytes=32 * MIB),
        name="pack",
    )(*(pltpu.with_memory_space_constraint(a, pltpu.HBM) for a in (expert_ids.T, tokens)))


def plan_kernel(ids_ref, gate_ref, weight_ref):
    tok_rows, route_count = ids_ref.shape
    block_rows = weight_ref.shape[2]
    experts = block_rows // ROWS
    gates = gate_ref[...]
    mix = gates / jnp.sum(gates, axis=1, keepdims=True)
    slot = slots_of(ids_ref[...], experts)
    expert_of = iota((tok_rows, experts), 1)
    mix_of = jnp.zeros((tok_rows, experts), jnp.float32)
    for k in range(route_count):
        mix_of = mix_of + jnp.where(ids_ref[:, k : k + 1] == expert_of, mix[:, k : k + 1], 0.0)
    repeat = jnp.where(
        iota((experts, block_rows), 1) // ROWS == iota((experts, block_rows), 0), 1.0, 0.0
    ).astype(jnp.bfloat16)
    slot = jnp.dot(slot.astype(jnp.bfloat16), repeat, preferred_element_type=jnp.float32)
    mix = jnp.dot(mix_of.astype(jnp.bfloat16), repeat, preferred_element_type=jnp.float32)
    row = iota(slot.shape, 1) % ROWS
    own = jnp.where((row < SLOTS) & (slot == row.astype(jnp.float32)), mix, 0.0)
    own = own.astype(weight_ref.dtype)
    for g in range(SLOTS):
        weight_ref[g, :tok_rows] = own
        here = jnp.where(slot == float(g), mix, 0.0)
        for i in range(EXTRA):
            weight_ref[g, (1 + i) * tok_rows : (2 + i) * tok_rows] = jnp.where(
                row == SLOTS + i, here, 0.0
            ).astype(weight_ref.dtype)


def plan(expert_ids, gate_weights, experts):
    shape = (SLOTS, (1 + EXTRA) * expert_ids.shape[0], experts * ROWS)
    return pl.pallas_call(
        plan_kernel,
        out_shape=pltpu.HBM(shape, jnp.bfloat16),
        compiler_params=pltpu.CompilerParams(vmem_limit_bytes=16 * MIB),
        cost_estimate=pl.CostEstimate(flops=10**8, bytes_accessed=10**6, transcendentals=0),
        name="plan",
    )(expert_ids, gate_weights)


def dequant_kernel(place, scale_ref, weight_ref, out_ref):
    row_blocks, col_blocks = (n // QBLK for n in weight_ref.shape)
    step = pl.program_id(0)
    for i in range(row_blocks):
        rows = slice(i * QBLK, (i + 1) * QBLK)
        for j in range(col_blocks):
            scale = scale_ref[step * row_blocks + i, j]
            scaled = weight_ref[rows, j * QBLK : (j + 1) * QBLK].astype(jnp.float32) * scale
            out_ref[rows, place(j) * QBLK : (place(j) + 1) * QBLK] = scaled.astype(out_ref.dtype)


def dequant(weight, scales, rows, place):
    row_count, col_count = weight.shape
    block = pl.BlockSpec((rows, col_count), lambda i: (i, 0))
    return pl.pallas_call(
        functools.partial(dequant_kernel, place),
        grid=(row_count // rows,),
        out_shape=pltpu.HBM(weight.shape, weight.dtype),
        in_specs=[pl.BlockSpec(memory_space=pltpu.SMEM), block],
        out_specs=block,
        compiler_params=pltpu.CompilerParams(vmem_limit_bytes=16 * MIB),
        cost_estimate=pl.CostEstimate(
            flops=row_count * col_count, bytes_accessed=4 * row_count * col_count, transcendentals=0
        ),
        name="dequant",
    )(scales, pltpu.with_memory_space_constraint(weight, pltpu.HBM))


def expert_kernel(
    hidden_tile, given_ref, gu_given_ref, down_given_ref, out_ref,
    in_ref, gu_ref, down_ref, x_ref, hidden_ref, in_sem, gu_sem, down_sem,
):
    group_width = x_ref.shape[1] // ROWS
    runs, tiles = in_sem.shape[0], gu_sem.shape[0]
    span = in_ref.shape[0] // runs
    sources = span // ROWS
    kept = sources * SLOTS
    order = (*range(SLOTS - 1, ROWS), *range(SLOTS - 1))

    def group(g):
        return slice(g * group_width, (g + 1) * group_width)

    def run_rows(run, rows):
        return slice(run * rows, (run + 1) * rows)

    def copies(given, held, sem, places):
        return [
            pltpu.make_async_copy(given.at[p], held.at[p], sem.at[i]) for i, p in enumerate(places)
        ]

    in_copies = copies(given_ref, in_ref, in_sem, [(run_rows(r, span),) for r in range(runs)])
    gu_places = [(slice(None), run_rows(t, 2 * hidden_tile)) for t in range(tiles)]
    gu_copies = copies(gu_given_ref, gu_ref, gu_sem, gu_places)
    down_copies = copies(down_given_ref, down_ref, down_sem, [(slice(None), group(f)) for f in order])

    def turned(back):
        to, come = iota((span, span), 1 if back else 0), iota((span, span), 0 if back else 1)
        same = (to // sources == come % ROWS) & (to % sources == come // ROWS)
        return jnp.where(same, 1.0, 0.0).astype(jnp.bfloat16)

    for copy in in_copies + gu_copies[:1]:
        copy.start()
    unpack = turned(False)
    for run in range(runs):
        in_copies[run].wait()
        for g in range(SLOTS):
            moved = jnp.dot(
                unpack, in_ref[run_rows(run, span), group(g)], preferred_element_type=jnp.float32
            ).astype(x_ref.dtype)
            for row in range(ROWS):
                slot, feature = (row, g) if row < SLOTS else (g, row)
                first = run * kept + slot * sources
                x_ref[first : first + sources, group(feature)] = moved[run_rows(row, sources)]
    for tile in range(tiles):
        gu_copies[tile].wait()
        for copy in gu_copies[tile + 1 : tile + 2] + down_copies[
            tile * ROWS // tiles : (tile + 1) * ROWS // tiles
        ]:
            copy.start()
        pre = jnp.dot(x_ref[...], gu_ref[gu_places[tile]], preferred_element_type=jnp.float32)
        gate, up = pre[:, :hidden_tile], pre[:, hidden_tile:]
        half = 0.5 * gate
        hidden_ref[:, run_rows(tile, hidden_tile)] = (half * (1.0 + jnp.tanh(half)) * up).astype(
            hidden_ref.dtype
        )
    pack_again = turned(True)

    def product(first, count):
        cols = slice(first * group_width, (first + count) * group_width)
        return jnp.dot(
            hidden_ref[...], down_ref[:, cols], preferred_element_type=jnp.float32
        ).astype(x_ref.dtype)

    def give(feature, result):
        for run in range(runs):
            first = run * kept + feature * sources
            gathered = jnp.concatenate(
                [result[run_rows(run, kept)]]
                + [x_ref[first : first + sources, group(f)] for f in range(SLOTS, ROWS)],
                axis=0,
            )
            out_ref[run_rows(run, span), group(feature)] = jnp.dot(
                pack_again, gathered, preferred_element_type=jnp.float32
            ).astype(out_ref.dtype)

    for copy in down_copies[:EXTRA + 1]:
        copy.wait()
    result = product(SLOTS - 1, EXTRA + 1)
    x_ref[:, SLOTS * group_width :] = result[:, group_width:]
    give(SLOTS - 1, result[:, :group_width])
    for copy in down_copies[EXTRA + 1 :]:
        copy.wait()
    for feature in range(0, SLOTS - 1, 2):
        result = product(feature, 2)
        give(feature, result[:, :group_width])
        give(feature + 1, result[:, group_width:])


def expert(arrived, gate_up, down, hidden_tile):
    block_rows, packed_width = arrived.shape
    feat_width, hidden_width = gate_up.shape[0], down.shape[0]
    live_rows = block_rows // ROWS * SLOTS
    runs = block_rows // 256
    tiles = hidden_width // hidden_tile
    given = pl.BlockSpec(memory_space=pl.ANY)

    return pl.pallas_call(
        functools.partial(expert_kernel, hidden_tile),
        out_shape=pltpu.VMEM(arrived.shape, arrived.dtype),
        in_specs=[given, given, given],
        out_specs=pl.BlockSpec(memory_space=pltpu.VMEM),
        scratch_shapes=[
            pltpu.VMEM(arrived.shape, jnp.bfloat16),
            pltpu.VMEM(gate_up.shape, jnp.bfloat16),
            pltpu.VMEM(down.shape, jnp.bfloat16),
            pltpu.VMEM((live_rows, feat_width), jnp.bfloat16),
            pltpu.VMEM((live_rows, hidden_width), jnp.bfloat16),
            pltpu.SemaphoreType.DMA((runs,)),
            pltpu.SemaphoreType.DMA((tiles,)),
            pltpu.SemaphoreType.DMA((ROWS,)),
        ],
        compiler_params=pltpu.CompilerParams(vmem_limit_bytes=48 * MIB),
        cost_estimate=pl.CostEstimate(
            flops=2 * live_rows * 3 * feat_width * hidden_width,
            bytes_accessed=6 * feat_width * hidden_width + 4 * block_rows * packed_width,
            transcendentals=live_rows * hidden_width,
        ),
        name="expert",
    )(*(pltpu.with_memory_space_constraint(a, pltpu.HBM) for a in (arrived, gate_up, down)))


def combine_kernel(weight_ref, in_ref, out_ref):
    tok_rows, feat_width = out_ref.shape
    group_width = feat_width // ROWS

    def group(g):
        return slice(g * group_width, (g + 1) * group_width)

    total = jnp.zeros((EXTRA * tok_rows, group_width), jnp.float32)
    for g in range(SLOTS):
        part = jnp.dot(weight_ref[g], in_ref[:, group(g)], preferred_element_type=jnp.float32)
        out_ref[:, group(g)] = part[:tok_rows].astype(out_ref.dtype)
        total = total + part[tok_rows:]
    for i in range(EXTRA):
        out_ref[:, group(SLOTS + i)] = total[i * tok_rows : (i + 1) * tok_rows].astype(out_ref.dtype)


def combine(weights, returned, out_shape):
    held = pl.BlockSpec(memory_space=pltpu.VMEM)
    return pl.pallas_call(
        combine_kernel,
        out_shape=out_shape,
        in_specs=[held, held],
        out_specs=held,
        compiler_params=pltpu.CompilerParams(vmem_limit_bytes=24 * MIB),
        name="combine",
    )(*(pltpu.with_memory_space_constraint(a, pltpu.VMEM) for a in (weights, returned)))


def exchange(blocks, experts):
    shape = blocks.shape
    moved = lax.all_to_all(
        blocks.reshape(experts, ROWS, shape[1]),
        ("expert", "helper"),
        split_axis=0,
        concat_axis=0,
        tiled=True,
    )
    return moved.reshape(shape)


def shards(tokens, expert_ids, gate_weights, w_gate_up, gu_scales, w_down, down_scales):
    experts = lax.axis_size("expert") * lax.axis_size("helper")
    hidden_width = w_down.shape[1]
    tile = 256
    arrived = exchange(pack(tokens, expert_ids, experts), experts)
    wide = tile // QBLK

    def place(j):
        part, block = divmod(j, hidden_width // QBLK)
        return block // wide * 2 * wide + part * wide + block % wide

    gate_up = dequant(w_gate_up[0], gu_scales[0], 256, place)
    down = dequant(w_down[0], down_scales[0], 128, lambda j: j)
    planned = plan(expert_ids, gate_weights, experts)
    arrived, planned = lax.optimization_barrier((arrived, planned))
    returned = exchange(expert(arrived, gate_up, down, tile), experts)
    return combine(planned, returned, jax.ShapeDtypeStruct(tokens.shape, tokens.dtype))


def solution(mesh):
    rows = ("expert", "helper")
    placed = (P(rows, None),) * 3 + (P(rows, None, None),) * 4
    return jax.shard_map(
        shards, mesh=mesh, in_specs=placed, out_specs=P(rows, None), check_vma=False
    )
```

```python
import functools

import jax
import jax.numpy as jnp
from jax import lax
from jax.experimental import pallas as pl
from jax.experimental.pallas import tpu as pltpu
from jax.sharding import PartitionSpec as P

QBLK = 128
SLOTS = 5
ROWS = 8
EXTRA = ROWS - SLOTS
MIB = 1 << 20


def iota(shape, dim):
    return lax.broadcasted_iota(jnp.int32, shape, dim)


def slots_of(ids, experts):
    tok_rows, route_count = ids.shape
    expert_of = iota((tok_rows, experts), 1)
    hit = jnp.zeros((tok_rows, experts), jnp.float32)
    for k in range(route_count):
        hit = hit + jnp.where(ids[:, k : k + 1] == expert_of, 1.0, 0.0)
    earlier = jnp.where(iota((tok_rows, tok_rows), 0) > iota((tok_rows, tok_rows), 1), 1.0, 0.0)
    rank = jnp.dot(
        earlier.astype(jnp.bfloat16), hit.astype(jnp.bfloat16), preferred_element_type=jnp.float32
    )
    return jnp.where(hit > 0.5, rank, -1.0)


def slots_for(ids, experts):
    route_count, tok_rows = ids.shape
    expert_of = iota((experts, tok_rows), 0)
    hit = jnp.zeros((experts, tok_rows), jnp.float32)
    for k in range(route_count):
        hit = hit + jnp.where(ids[k : k + 1, :] == expert_of, 1.0, 0.0)
    earlier = jnp.where(iota((tok_rows, tok_rows), 0) < iota((tok_rows, tok_rows), 1), 1.0, 0.0)
    rank = jnp.dot(
        hit.astype(jnp.bfloat16), earlier.astype(jnp.bfloat16), preferred_element_type=jnp.float32
    )
    return jnp.where(hit > 0.5, rank, -1.0)


ALWAYS, SHARED, NEVER = 99.0, -2, -3


def pack_kernel(
    ids_given_ref, given_ref, out_ref, ids_ref, tok_ref, block_ref, slot_ref, ids_sem, tok_sem, out_sem
):
    tok_rows, feat_width = tok_ref.shape
    group_width = feat_width // ROWS
    block_rows = block_ref.shape[0]
    experts = block_rows // ROWS
    parts = 1 + EXTRA
    fetch_ids = pltpu.make_async_copy(ids_given_ref, ids_ref, ids_sem)
    fetch_ids.start()
    fetch = pltpu.make_async_copy(given_ref, tok_ref, tok_sem)
    fetch.start()
    repeat = jnp.where(
        iota((block_rows, experts), 0) // ROWS == iota((block_rows, experts), 1), 1.0, 0.0
    ).astype(jnp.bfloat16)
    shape = (block_rows, parts * tok_rows)
    row = iota(shape, 0) % ROWS
    part = iota(shape, 1) // tok_rows
    own = (part == 0) & (row < SLOTS)
    shared = (part > 0) & (row == SLOTS - 1 + part)
    slot_ref[...] = jnp.where(own, row, jnp.where(shared, SHARED, NEVER)).astype(jnp.float32)

    fetch_ids.wait()
    slot = slots_for(ids_ref[...], experts).astype(jnp.bfloat16)
    spread = jnp.dot(
        repeat, jnp.concatenate([slot] * parts, axis=1), preferred_element_type=jnp.float32
    )
    wanted = slot_ref[...]
    slot_ref[...] = jnp.where(
        wanted == spread, ALWAYS, jnp.where(wanted == float(SHARED), spread, -1.0)
    )
    fetch.wait()

    def group(g):
        return slice(g * group_width, (g + 1) * group_width)

    writes = []
    for g in range(SLOTS):
        code = slot_ref[...]
        chosen = jnp.where((code == ALWAYS) | (code == float(g)), 1.0, 0.0).astype(jnp.bfloat16)
        source = jnp.concatenate(
            [tok_ref[:, group(f)] for f in (g, *range(SLOTS, ROWS))], axis=0
        )
        block_ref[:, group(g)] = jnp.dot(
            chosen, source, preferred_element_type=jnp.float32
        ).astype(block_ref.dtype)
        writes.append(
            pltpu.make_async_copy(block_ref.at[:, group(g)], out_ref.at[:, group(g)], out_sem.at[g])
        )
        writes[-1].start()
    for write in writes:
        write.wait()


def pack(tokens, expert_ids, experts):
    tok_rows, feat_width = tokens.shape
    shape = (experts * ROWS, feat_width // ROWS * SLOTS)
    return pl.pallas_call(
        pack_kernel,
        out_shape=pltpu.HBM(shape, tokens.dtype),
        in_specs=[pl.BlockSpec(memory_space=pl.ANY)] * 2,
        out_specs=pl.BlockSpec(memory_space=pl.ANY),
        scratch_shapes=[
            pltpu.VMEM(expert_ids.shape[::-1], expert_ids.dtype),
            pltpu.VMEM(tokens.shape, tokens.dtype),
            pltpu.VMEM(shape, tokens.dtype),
            pltpu.VMEM((shape[0], (1 + EXTRA) * tok_rows), jnp.float32),
            pltpu.SemaphoreType.DMA,
            pltpu.SemaphoreType.DMA,
            pltpu.SemaphoreType.DMA((SLOTS,)),
        ],
        compiler_params=pltpu.CompilerParams(vmem_limit_bytes=32 * MIB),
        name="pack",
    )(*(pltpu.with_memory_space_constraint(a, pltpu.HBM) for a in (expert_ids.T, tokens)))


def plan_kernel(ids_ref, gate_ref, weight_ref):
    tok_rows, route_count = ids_ref.shape
    block_rows = weight_ref.shape[2]
    experts = block_rows // ROWS
    gates = gate_ref[...]
    mix = gates / jnp.sum(gates, axis=1, keepdims=True)
    slot = slots_of(ids_ref[...], experts)
    expert_of = iota((tok_rows, experts), 1)
    mix_of = jnp.zeros((tok_rows, experts), jnp.float32)
    for k in range(route_count):
        mix_of = mix_of + jnp.where(ids_ref[:, k : k + 1] == expert_of, mix[:, k : k + 1], 0.0)
    repeat = jnp.where(
        iota((experts, block_rows), 1) // ROWS == iota((experts, block_rows), 0), 1.0, 0.0
    ).astype(jnp.bfloat16)
    slot = jnp.dot(slot.astype(jnp.bfloat16), repeat, preferred_element_type=jnp.float32)
    mix = jnp.dot(mix_of.astype(jnp.bfloat16), repeat, preferred_element_type=jnp.float32)
    row = iota(slot.shape, 1) % ROWS
    own = jnp.where((row < SLOTS) & (slot == row.astype(jnp.float32)), mix, 0.0)
    own = own.astype(weight_ref.dtype)
    for g in range(SLOTS):
        weight_ref[g, :tok_rows] = own
        here = jnp.where(slot == float(g), mix, 0.0)
        for i in range(EXTRA):
            weight_ref[g, (1 + i) * tok_rows : (2 + i) * tok_rows] = jnp.where(
                row == SLOTS + i, here, 0.0
            ).astype(weight_ref.dtype)


def plan(expert_ids, gate_weights, experts):
    shape = (SLOTS, (1 + EXTRA) * expert_ids.shape[0], experts * ROWS)
    return pl.pallas_call(
        plan_kernel,
        out_shape=pltpu.HBM(shape, jnp.bfloat16),
        compiler_params=pltpu.CompilerParams(vmem_limit_bytes=16 * MIB),
        cost_estimate=pl.CostEstimate(flops=10**8, bytes_accessed=10**6, transcendentals=0),
        name="plan",
    )(expert_ids, gate_weights)


def dequant_kernel(place, scale_ref, weight_ref, out_ref):
    row_blocks, col_blocks = (n // QBLK for n in weight_ref.shape)
    step = pl.program_id(0)
    for i in range(row_blocks):
        rows = slice(i * QBLK, (i + 1) * QBLK)
        for j in range(col_blocks):
            scale = scale_ref[step * row_blocks + i, j]
            scaled = weight_ref[rows, j * QBLK : (j + 1) * QBLK].astype(jnp.float32) * scale
            out_ref[rows, place(j) * QBLK : (place(j) + 1) * QBLK] = scaled.astype(out_ref.dtype)


def dequant(weight, scales, rows, place):
    row_count, col_count = weight.shape
    block = pl.BlockSpec((rows, col_count), lambda i: (i, 0))
    return pl.pallas_call(
        functools.partial(dequant_kernel, place),
        grid=(row_count // rows,),
        out_shape=pltpu.HBM(weight.shape, weight.dtype),
        in_specs=[pl.BlockSpec(memory_space=pltpu.SMEM), block],
        out_specs=block,
        compiler_params=pltpu.CompilerParams(vmem_limit_bytes=16 * MIB),
        cost_estimate=pl.CostEstimate(
            flops=row_count * col_count, bytes_accessed=4 * row_count * col_count, transcendentals=0
        ),
        name="dequant",
    )(scales, pltpu.with_memory_space_constraint(weight, pltpu.HBM))


def expert_kernel(
    hidden_tile, given_ref, gu_given_ref, down_given_ref, out_ref,
    in_ref, gu_ref, down_ref, x_ref, hidden_ref, in_sem, gu_sem, down_sem,
):
    group_width = x_ref.shape[1] // ROWS
    runs, tiles = in_sem.shape[0], gu_sem.shape[0]
    span = in_ref.shape[0] // runs
    sources = span // ROWS
    kept = sources * SLOTS
    order = (*range(SLOTS - 1, ROWS), *range(SLOTS - 1))

    def group(g):
        return slice(g * group_width, (g + 1) * group_width)

    def run_rows(run, rows):
        return slice(run * rows, (run + 1) * rows)

    def copies(given, held, sem, places):
        return [
            pltpu.make_async_copy(given.at[p], held.at[p], sem.at[i]) for i, p in enumerate(places)
        ]

    in_copies = copies(given_ref, in_ref, in_sem, [(run_rows(r, span),) for r in range(runs)])
    gu_places = [(slice(None), run_rows(t, 2 * hidden_tile)) for t in range(tiles)]
    gu_copies = copies(gu_given_ref, gu_ref, gu_sem, gu_places)
    down_copies = copies(down_given_ref, down_ref, down_sem, [(slice(None), group(f)) for f in order])

    def turned(back):
        to, come = iota((span, span), 1 if back else 0), iota((span, span), 0 if back else 1)
        same = (to // sources == come % ROWS) & (to % sources == come // ROWS)
        return jnp.where(same, 1.0, 0.0).astype(jnp.bfloat16)

    for copy in in_copies + gu_copies[:1]:
        copy.start()
    unpack = turned(False)
    for run in range(runs):
        in_copies[run].wait()
        for g in range(SLOTS):
            moved = jnp.dot(
                unpack, in_ref[run_rows(run, span), group(g)], preferred_element_type=jnp.float32
            ).astype(x_ref.dtype)
            for row in range(ROWS):
                slot, feature = (row, g) if row < SLOTS else (g, row)
                first = run * kept + slot * sources
                x_ref[first : first + sources, group(feature)] = moved[run_rows(row, sources)]
    for tile in range(tiles):
        gu_copies[tile].wait()
        for copy in gu_copies[tile + 1 : tile + 2] + down_copies[
            tile * ROWS // tiles : (tile + 1) * ROWS // tiles
        ]:
            copy.start()
        pre = jnp.dot(x_ref[...], gu_ref[gu_places[tile]], preferred_element_type=jnp.float32)
        gate, up = pre[:, :hidden_tile], pre[:, hidden_tile:]
        half = 0.5 * gate
        hidden_ref[:, run_rows(tile, hidden_tile)] = (half * (1.0 + jnp.tanh(half)) * up).astype(
            hidden_ref.dtype
        )
    pack_again = turned(True)

    def product(first, count):
        cols = slice(first * group_width, (first + count) * group_width)
        return jnp.dot(
            hidden_ref[...], down_ref[:, cols], preferred_element_type=jnp.float32
        ).astype(x_ref.dtype)

    def give(feature, result):
        for run in range(runs):
            first = run * kept + feature * sources
            gathered = jnp.concatenate(
                [result[run_rows(run, kept)]]
                + [x_ref[first : first + sources, group(f)] for f in range(SLOTS, ROWS)],
                axis=0,
            )
            out_ref[run_rows(run, span), group(feature)] = jnp.dot(
                pack_again, gathered, preferred_element_type=jnp.float32
            ).astype(out_ref.dtype)

    for copy in down_copies[: EXTRA + 1]:
        copy.wait()
    result = product(SLOTS - 1, EXTRA + 1)
    x_ref[:, SLOTS * group_width :] = result[:, group_width:]
    held = [(SLOTS - 1, result[:, :group_width])]
    for copy in down_copies[EXTRA + 1 :]:
        copy.wait()
    for feature in range(0, SLOTS - 1, 2):
        result = product(feature, 2)
        for done in held:
            give(*done)
        held = [(feature, result[:, :group_width]), (feature + 1, result[:, group_width:])]
    for done in held:
        give(*done)


def expert(arrived, gate_up, down, hidden_tile):
    block_rows, packed_width = arrived.shape
    feat_width, hidden_width = gate_up.shape[0], down.shape[0]
    live_rows = block_rows // ROWS * SLOTS
    runs = block_rows // 256
    tiles = hidden_width // hidden_tile
    given = pl.BlockSpec(memory_space=pl.ANY)

    return pl.pallas_call(
        functools.partial(expert_kernel, hidden_tile),
        out_shape=pltpu.VMEM(arrived.shape, arrived.dtype),
        in_specs=[given, given, given],
        out_specs=pl.BlockSpec(memory_space=pltpu.VMEM),
        scratch_shapes=[
            pltpu.VMEM(arrived.shape, jnp.bfloat16),
            pltpu.VMEM(gate_up.shape, jnp.bfloat16),
            pltpu.VMEM(down.shape, jnp.bfloat16),
            pltpu.VMEM((live_rows, feat_width), jnp.bfloat16),
            pltpu.VMEM((live_rows, hidden_width), jnp.bfloat16),
            pltpu.SemaphoreType.DMA((runs,)),
            pltpu.SemaphoreType.DMA((tiles,)),
            pltpu.SemaphoreType.DMA((ROWS,)),
        ],
        compiler_params=pltpu.CompilerParams(vmem_limit_bytes=48 * MIB),
        cost_estimate=pl.CostEstimate(
            flops=2 * live_rows * 3 * feat_width * hidden_width,
            bytes_accessed=6 * feat_width * hidden_width + 4 * block_rows * packed_width,
            transcendentals=live_rows * hidden_width,
        ),
        name="expert",
    )(*(pltpu.with_memory_space_constraint(a, pltpu.HBM) for a in (arrived, gate_up, down)))


def combine_kernel(weight_ref, in_ref, out_ref):
    tok_rows, feat_width = out_ref.shape
    group_width = feat_width // ROWS

    def group(g):
        return slice(g * group_width, (g + 1) * group_width)

    total = jnp.zeros((EXTRA * tok_rows, group_width), jnp.float32)
    for g in range(SLOTS):
        part = jnp.dot(weight_ref[g], in_ref[:, group(g)], preferred_element_type=jnp.float32)
        out_ref[:, group(g)] = part[:tok_rows].astype(out_ref.dtype)
        total = total + part[tok_rows:]
    for i in range(EXTRA):
        out_ref[:, group(SLOTS + i)] = total[i * tok_rows : (i + 1) * tok_rows].astype(out_ref.dtype)


def combine(weights, returned, out_shape):
    held = pl.BlockSpec(memory_space=pltpu.VMEM)
    return pl.pallas_call(
        combine_kernel,
        out_shape=out_shape,
        in_specs=[held, held],
        out_specs=held,
        compiler_params=pltpu.CompilerParams(vmem_limit_bytes=24 * MIB),
        name="combine",
    )(*(pltpu.with_memory_space_constraint(a, pltpu.VMEM) for a in (weights, returned)))


def exchange(blocks, experts):
    shape = blocks.shape
    moved = lax.all_to_all(
        blocks.reshape(experts, ROWS, shape[1]),
        ("expert", "helper"),
        split_axis=0,
        concat_axis=0,
        tiled=True,
    )
    return moved.reshape(shape)


def shards(tokens, expert_ids, gate_weights, w_gate_up, gu_scales, w_down, down_scales):
    experts = lax.axis_size("expert") * lax.axis_size("helper")
    hidden_width = w_down.shape[1]
    tile = 256
    arrived = exchange(pack(tokens, expert_ids, experts), experts)
    wide = tile // QBLK

    def place(j):
        part, block = divmod(j, hidden_width // QBLK)
        return block // wide * 2 * wide + part * wide + block % wide

    gate_up = dequant(w_gate_up[0], gu_scales[0], 256, place)
    down = dequant(w_down[0], down_scales[0], 128, lambda j: j)
    planned = plan(expert_ids, gate_weights, experts)
    arrived, planned = lax.optimization_barrier((arrived, planned))
    returned = exchange(expert(arrived, gate_up, down, tile), experts)
    return combine(planned, returned, jax.ShapeDtypeStruct(tokens.shape, tokens.dtype))


def solution(mesh):
    rows = ("expert", "helper")
    placed = (P(rows, None),) * 3 + (P(rows, None, None),) * 4
    return jax.shard_map(
        shards, mesh=mesh, in_specs=placed, out_specs=P(rows, None), check_vma=False
    )
```
